32 devices in a mesh: row: 8 (over z, x), col: 4 (over y, core).
Axes of the slice: x: 2, y: 2, z: 4, core: 2. Of those that a mesh axis runs over, the one named last changes fastest.
Arguments:
- cotangent: bfloat16 [1536, 1536], P('row', 'col'), may hold values from -9 to 9, as said below
- saved_panels: bfloat16 [3, 1536, 256], P(None, ('row', 'col')), may hold values from -0.15625 to 0.15625
- upstream: bfloat16 [3, 1536, 256], P(None, ('row', 'col')), may hold values from -6 to 6
- inverse_diag: float32 [3, 256, 256], replicated, as said below
- panel_tops: bfloat16 [3, 256, 256], replicated, may hold values from -0.375 to 0.375
Outputs:
- columns: bfloat16 [3, 1536, 256], P(None, ('row', 'col'))
- diag_cot: float32 [3, 256, 256], replicated
The draws below stay inside these ranges and needn't reach their ends.
Inputs may be any that keep to these rules, and one draw needn't show every extreme that they name: `cotangent`: symmetric once its columns are reordered as in the first step. `inverse_diag`: each matrix is lower triangular with a diagonal of 0.6 to 1.2.
All inputs are finite; a program needn't handle non-finite values.
Results may differ from the reference program's by a relative error of at most 0.02.
Values may be sent and summed in bfloat16 or wider, within the bound.
No kernel may reach another device: no remote copies, remote signals or barrier semaphores. Data moves between devices by JAX's collectives and lax.ppermute only.
A program may use at most 64 MiB of HBM per device.

```python
import jax
import jax.numpy as jnp
from jax import lax

B = 256
NPANEL = 3
TB = 48
PERIOD = 4
GROUPS = 8
ORDER = 1536


def draw_cotangent(key, part):
    base = jnp.clip(jax.random.normal(key, (ORDER, ORDER), jnp.float32), -6.0, 6.0)
    symmetric = (base + base.T) * 0.7071
    stored = symmetric.reshape(ORDER, GROUPS, PERIOD, TB).transpose(0, 2, 1, 3).reshape(ORDER, ORDER)
    return stored.astype(jnp.bfloat16)


def draw_inverse_diag(key, part):
    first = jax.random.fold_in(key, 11)
    second = jax.random.fold_in(key, 12)
    spread = jnp.clip(jax.random.normal(first, (NPANEL, B, B), jnp.float32), -4.0, 4.0)
    spread = spread / jnp.sqrt(jnp.float32(B))
    middle = jax.random.uniform(second, (NPANEL, B), jnp.float32, 0.6, 1.2)
    identity = jnp.eye(B, dtype=jnp.float32)
    return jnp.tril(spread, -1) + middle[:, :, None] * identity[None, :, :]


def block_scale(stream_key, shape, shards, least, high):
    gain, own = 1.0, jax.random.fold_in(stream_key, 6)
    for position, shards_of in shards:
        draws = jnp.exp(jax.random.uniform(jax.random.fold_in(own, position), (shards_of,), jnp.float32, least / len(shards), high / len(shards)))
        gain = gain * jnp.repeat(draws, shape[position] // shards_of).reshape([-1 if axis == position else 1 for axis in range(len(shape))])
    return gain


def scatter_about(key, dims, scale, bound, pieces=(), kind=jnp.bfloat16):
    values = scale * jax.random.normal(key, dims, jnp.float32)
    if pieces:
        values = values * block_scale(key, dims, pieces, -0.22, 0.18)
    return jnp.clip(values, -bound, bound).astype(kind)


def setup_inputs(seed: int = 0) -> dict:
    key_list = jax.random.split(jax.random.key(seed), 6)
    cotangent = draw_cotangent(jax.random.fold_in(key_list[5], 71), 0)
    saved_panels = scatter_about(key_list[1], (NPANEL, ORDER, B), ORDER ** -0.5, 0.15625, ((1, 32),))
    upstream = scatter_about(key_list[2], (NPANEL, ORDER, B), 1.0, 6.0, ((1, 32),))
    inverse_diag = draw_inverse_diag(jax.random.fold_in(key_list[5], 71), 0)
    panel_tops = scatter_about(key_list[4], (NPANEL, B, B), B ** -0.5, 0.375)
    return {"cotangent": cotangent, "saved_panels": saved_panels, "upstream": upstream, "inverse_diag": inverse_diag, "panel_tops": panel_tops}


def reference(cotangent, saved_panels, upstream, inverse_diag, panel_tops):
    highest = lax.Precision.HIGHEST
    reordered = saved_panels.reshape(NPANEL, GROUPS, PERIOD, TB, B).transpose(0, 2, 1, 3, 4).reshape(NPANEL, ORDER, B)
    joined = jnp.concatenate([reordered[index] for index in range(NPANEL)], axis=1)

    def block_product(block):
        return jnp.dot(block, joined, preferred_element_type=jnp.float32)

    resident = lax.map(block_product, cotangent.reshape(GROUPS, TB * PERIOD, ORDER)).reshape(ORDER, NPANEL * B)
    columns_list = []
    diag_list = []
    for index in range(NPANEL):
        panel = saved_panels[index]
        product = resident[:, index * B:(index + 1) * B]
        for earlier in range(index):
            product = product + jnp.dot(columns_list[earlier], panel_tops[index * (index - 1) // 2 + earlier], preferred_element_type=jnp.float32)
        combined = upstream[index].astype(jnp.float32) - 2.0 * product
        columns_now = jnp.dot(combined, inverse_diag[index], precision=highest, preferred_element_type=jnp.float32).astype(jnp.bfloat16)
        gram = jnp.dot(panel.T, columns_now, preferred_element_type=jnp.float32)
        result = -gram
        for earlier in range(index):
            cross = jnp.dot(columns_list[earlier].T, panel, preferred_element_type=jnp.float32)
            solved = jnp.dot(cross, inverse_diag[index], precision=highest, preferred_element_type=jnp.float32)
            tops = panel_tops[index * (index - 1) // 2 + earlier].astype(jnp.float32)
            result = result + 2.0 * jnp.dot(tops.T, solved, precision=highest, preferred_element_type=jnp.float32)
        columns_list.append(columns_now)
        diag_list.append(result)
    return jnp.stack(columns_list), jnp.stack(diag_list)
```

```python
import functools

import jax
import jax.numpy as jnp
from jax import lax
from jax.experimental import pallas as pl
from jax.experimental.pallas import tpu as pltpu
from jax.sharding import PartitionSpec as P

F32 = jnp.float32
BF16 = jnp.bfloat16
VMEM = pl.BlockSpec(memory_space=pltpu.VMEM)


def swap(value, axes, sizes, bits):
    dims = [sizes[axis] for axis in axes]
    pairs = []
    count = 1
    for dim in dims:
        count *= dim
    for source in range(count):
        rest, coords = source, []
        for dim in reversed(dims):
            coords.append(rest % dim)
            rest //= dim
        coords = coords[::-1]
        target = 0
        for axis, dim, coord in zip(axes, dims, coords):
            target = target * dim + (coord ^ bits.get(axis, 0))
        pairs.append((source, target))
    return lax.ppermute(value, axes, pairs)


def split(value):
    high = value.astype(BF16)
    return high, (value - high.astype(F32)).astype(BF16)


def dot(left, right):
    return jnp.dot(left, right, preferred_element_type=F32)


def dot_rows(left, right):
    return lax.dot_general(left, right, (((0,), (0,)), ((), ())), preferred_element_type=F32)


def product_kernel(order, cols, *refs):
    cot_ref, tiles, outs = refs[0], refs[1 : 1 + len(order)], refs[1 + len(order) : -2]
    joined, total = refs[-2:]
    row, col = lax.axis_index("row"), lax.axis_index("col")
    for bits_list, ref in zip(order, tiles):
        for place, bits in enumerate(bits_list):
            panels, height, width = ref.shape[-3:]
            start = pl.multiple_of((row ^ bits) * height, height)
            for panel in range(panels):
                joined[pl.ds(start, height), panel * width : (panel + 1) * width] = ref[place, panel]
    total[...] = dot(cot_ref[...], joined[...])
    height = outs[0].shape[0]
    for bits in range(cols):
        start = pl.multiple_of((col ^ bits) * height, height)
        outs[bits][...] = total[pl.ds(start, height), :].astype(outs[bits].dtype)


def panels_kernel(cols, *refs):
    parts, refs = refs[:cols], refs[cols:]
    saved_ref, upstream_ref, solver_ref, tops_ref, columns_ref, keep_ref, send_ref, diag = refs
    panels, height, width = saved_ref.shape
    product = parts[0][...]
    for part in parts[1:]:
        product = product + part[...].astype(F32)
    columns = []
    for index in range(panels):
        panel = saved_ref[index]
        appended = None
        for earlier in range(index):
            term = dot(columns[earlier], tops_ref[index * (index - 1) // 2 + earlier])
            appended = term if appended is None else appended + term
        summed = product[:, index * width : (index + 1) * width]
        if appended is not None:
            summed = summed + appended
        combined = upstream_ref[index].astype(F32) - 2.0 * summed
        high, low = split(combined)
        solver_high, solver_low = split(solver_ref[index])
        first = dot(jnp.concatenate([high, low, panel]), solver_high)
        second = dot(jnp.concatenate([high, panel]), solver_low)
        now = (first[:height] + (first[height : 2 * height] + second[:height])).astype(BF16)
        columns_ref[index] = now
        result = -dot_rows(panel, now)
        if appended is not None:
            solved_high, solved_low = split(2.0 * (first[2 * height :] + second[height:]))
            appended_high, appended_low = split(appended)
            result = result + dot_rows(
                jnp.concatenate([appended_high, appended_high, appended_low]),
                jnp.concatenate([solved_high, solved_low, solved_high]),
            )
        diag[index * width : (index + 1) * width, :] = result
        columns.append(now)
    piece = keep_ref.shape[1]
    core, spot = place_of()
    for bits in range(4):
        here = pl.multiple_of((core * 4 + (spot ^ bits)) * piece, piece)
        there = pl.multiple_of(((1 - core) * 4 + (spot ^ bits)) * piece, piece)
        keep_ref[bits] = diag[pl.ds(here, piece), :]
        send_ref[bits] = diag[pl.ds(there, piece), :].astype(BF16)


def place_of():
    row, col = lax.axis_index("row"), lax.axis_index("col")
    return col & 1, ((col >> 1) & 1) * 2 + (row & 1)


def finish_kernel(here_ref, there_ref, out_ref):
    core, spot = place_of()
    piece = here_ref.shape[1]
    for bits in range(4):
        here = pl.multiple_of((core * 4 + (spot ^ bits)) * piece, piece)
        there = pl.multiple_of(((1 - core) * 4 + (spot ^ bits)) * piece, piece)
        out_ref[pl.ds(here, piece), :] = here_ref[bits].astype(F32)
        out_ref[pl.ds(there, piece), :] = there_ref[bits].astype(F32)


def body(sizes, cotangent, saved_panels, upstream, inverse_diag, panel_tops):
    rows, cols = sizes["row"], sizes["col"]
    panels, height, width = saved_panels.shape
    limit = pltpu.CompilerParams(vmem_limit_bytes=32 * 1024 * 1024)

    order, tiles = [(0,)], [saved_panels[None]]
    far = [
        swap(saved_panels, ("row",), sizes, {"row": bits}) for bits in range(2, rows, 2)
    ]
    near = swap(saved_panels, ("row",), sizes, {"row": 1})
    order.append((1,))
    tiles.append(near[None])
    if far:
        for bits, value in zip(range(2, rows, 2), far):
            order.append((bits,))
            tiles.append(value[None])
        order.append(tuple(bits ^ 1 for bits in range(2, rows, 2)))
        tiles.append(swap(jnp.stack(far), ("row",), sizes, {"row": 1}))

    tall = cols * height
    parts = pl.pallas_call(
        functools.partial(product_kernel, order, cols),
        out_shape=[
            jax.ShapeDtypeStruct((height, panels * width), BF16 if bits else F32)
            for bits in range(cols)
        ],
        in_specs=[VMEM] * (1 + len(tiles)),
        out_specs=[VMEM] * cols,
        scratch_shapes=[
            pltpu.VMEM((rows * height, panels * width), BF16),
            pltpu.VMEM((tall, panels * width), F32),
        ],
        compiler_params=limit,
    )(cotangent, *tiles)

    parts = [parts[0]] + [
        swap(parts[bits], ("col",), sizes, {"col": bits}) for bits in range(1, cols)
    ]

    piece = panels * width // 8
    columns, keep, send = pl.pallas_call(
        functools.partial(panels_kernel, cols),
        out_shape=[
            jax.ShapeDtypeStruct(saved_panels.shape, BF16),
            jax.ShapeDtypeStruct((4, piece, width), F32),
            jax.ShapeDtypeStruct((4, piece, width), BF16),
        ],
        in_specs=[VMEM] * (cols + 4),
        out_specs=[VMEM] * 3,
        scratch_shapes=[pltpu.VMEM((panels * width, width), F32)],
        compiler_params=limit,
    )(*parts, saved_panels, upstream, inverse_diag, panel_tops)

    both = ("row", "col")
    half = keep + swap(send, ("col",), sizes, {"col": 1}).astype(F32)
    spots = [{"col": (bits >> 1) * 2, "row": bits & 1} for bits in range(4)]
    total = half[0]
    for bits in range(1, 4):
        total = total + swap(half[bits].astype(BF16), both, sizes, spots[bits]).astype(F32)
    others = [{"row": bits} for bits in (2**power for power in range(1, rows.bit_length() - 1))]
    others += [{"col": bits} for bits in (2**power for power in range(2, cols.bit_length() - 1))]
    if len(others) == 2 and "col" not in others[1]:
        mine = total.astype(BF16)
        first, second = others[0]["row"], others[1]["row"]
        from_first, from_second, from_both = [
            swap(mine, ("row",), sizes, {"row": bits}) for bits in (first, second, first ^ second)
        ]
        total = (mine.astype(F32) + from_first.astype(F32)) + (
            from_second.astype(F32) + from_both.astype(F32)
        )
    else:
        for bits in others:
            mine = total.astype(BF16)
            total = mine.astype(F32) + swap(mine, tuple(bits), sizes, bits).astype(F32)
    mine = total.astype(BF16)
    here = jnp.stack([mine] + [swap(mine, both, sizes, spots[bits]) for bits in range(1, 4)])
    there = swap(here, ("col",), sizes, {"col": 1})
    diag_cot = pl.pallas_call(
        finish_kernel,
        out_shape=jax.ShapeDtypeStruct((panels * width, width), F32),
        in_specs=[VMEM] * 2,
        out_specs=VMEM,
        compiler_params=limit,
    )(here, there)
    return columns, diag_cot.reshape(panels, width, width)


def solution(mesh):
    in_specs = (
        P("row", "col"),
        P(None, ("row", "col"), None),
        P(None, ("row", "col"), None),
        P(),
        P(),
    )
    out_specs = (P(None, ("row", "col"), None), P())
    return jax.shard_map(
        functools.partial(body, dict(mesh.shape)),
        mesh=mesh,
        in_specs=in_specs,
        out_specs=out_specs,
        check_vma=False,
    )
```

```python
import functools

import jax
import jax.numpy as jnp
from jax import lax
from jax.experimental import pallas as pl
from jax.experimental.pallas import tpu as pltpu
from jax.sharding import PartitionSpec as P

F32 = jnp.float32
BF16 = jnp.bfloat16
VMEM = pl.BlockSpec(memory_space=pltpu.VMEM)


def swap(value, axes, sizes, bits):
    dims = [sizes[axis] for axis in axes]
    pairs = []
    count = 1
    for dim in dims:
        count *= dim
    for source in range(count):
        rest, coords = source, []
        for dim in reversed(dims):
            coords.append(rest % dim)
            rest //= dim
        coords = coords[::-1]
        target = 0
        for axis, dim, coord in zip(axes, dims, coords):
            target = target * dim + (coord ^ bits.get(axis, 0))
        pairs.append((source, target))
    return lax.ppermute(value, axes, pairs)


def split(value):
    high = value.astype(BF16)
    return high, (value - high.astype(F32)).astype(BF16)


def dot(left, right):
    return jnp.dot(left, right, preferred_element_type=F32)


def dot_rows(left, right):
    return lax.dot_general(left, right, (((0,), (0,)), ((), ())), preferred_element_type=F32)


def prepare_kernel(cot_ref, saved_ref, upstream_ref, solver_ref, cot_out, saved_out, upstream_out, high_out, low_out):
    cot_out[...] = cot_ref[...]
    saved_out[...] = saved_ref[...]
    upstream_out[...] = upstream_ref[...]
    high, low = split(solver_ref[...])
    high_out[...] = high
    low_out[...] = low


def main_kernel(along_row, along_col, *refs):
    row_refs, refs = refs[: len(along_row)], refs[len(along_row) :]
    col_refs, refs = refs[: len(along_col)], refs[len(along_col) :]
    cot_ref, upstream_ref, high_ref, low_ref, tops_ref = refs[:5]
    columns_keep, columns_send, keep_ref, send_ref, joined, own, total, diag = refs[5:]
    row, col = lax.axis_index("row"), lax.axis_index("col")
    panels, height, width = upstream_ref.shape

    def place(target, index, tile):
        start = pl.multiple_of(index * height, height)
        for panel in range(panels):
            target[pl.ds(start, height), panel * width : (panel + 1) * width] = tile[panel]

    for bits_list, ref in zip(along_row, row_refs):
        for spot, bits in enumerate(bits_list):
            place(joined, row ^ bits, ref.at[spot])
    for bits_list, ref in zip(along_col, col_refs):
        for spot, bits in enumerate(bits_list):
            place(own, col ^ bits, ref.at[spot])
    total[...] = -2.0 * dot(cot_ref[...], joined[...])
    mine = pl.ds(pl.multiple_of(col * height, height), height)
    for index in range(panels):
        span = slice(index * width, (index + 1) * width)
        total[mine, span] += upstream_ref[index].astype(F32)

    columns = []
    tall = own.shape[0]
    for index in range(panels):
        span = slice(index * width, (index + 1) * width)
        panel = own[:, span]
        combined = total[:, span]
        appended = None
        for earlier in range(index):
            term = dot(columns[earlier], tops_ref[index * (index - 1) // 2 + earlier])
            appended = term if appended is None else appended + term
        if appended is not None:
            combined = combined - 2.0 * appended
        high, low = split(combined)
        if appended is None:
            first = dot(jnp.concatenate([high, low]), high_ref[index])
            second = dot(high, low_ref[index])
        else:
            first = dot(jnp.concatenate([high, low, panel]), high_ref[index])
            second = dot(jnp.concatenate([high, panel]), low_ref[index])
        now = first[:tall] + (first[tall : 2 * tall] + second[:tall])
        total[:, span] = now
        now = now.astype(BF16)
        columns.append(now)
        result = -dot_rows(panel, now)
        if appended is not None:
            solved = 2.0 * (first[2 * tall :] + second[tall:])
            result = result + dot_rows(appended.astype(BF16), solved.astype(BF16))
        diag[span, :] = result

    piece = keep_ref.shape[1]
    core, spot = place_of()
    for bits in range(4):
        here = pl.multiple_of((core * 4 + (spot ^ bits)) * piece, piece)
        there = pl.multiple_of(((1 - core) * 4 + (spot ^ bits)) * piece, piece)
        keep_ref[bits] = diag[pl.ds(here, piece), :]
        send_ref[bits] = diag[pl.ds(there, piece), :].astype(BF16)
    for pair in range(columns_keep.shape[0]):
        for bits, ref in ((2 * pair, columns_keep), (2 * pair + 1, columns_send)):
            tile = pl.ds(pl.multiple_of((col ^ bits) * height, height), height)
            for index in range(panels):
                ref[pair, index] = total[tile, index * width : (index + 1) * width].astype(ref.dtype)


def place_of():
    row, col = lax.axis_index("row"), lax.axis_index("col")
    return col & 1, ((col >> 1) & 1) * 2 + (row & 1)


def finish_kernel(here_ref, there_ref, out_ref):
    core, spot = place_of()
    piece = here_ref.shape[1]
    for bits in range(4):
        here = pl.multiple_of((core * 4 + (spot ^ bits)) * piece, piece)
        there = pl.multiple_of(((1 - core) * 4 + (spot ^ bits)) * piece, piece)
        out_ref[pl.ds(here, piece), :] = here_ref[bits].astype(F32)
        out_ref[pl.ds(there, piece), :] = there_ref[bits].astype(F32)


def after(value, *others):
    return lax.optimization_barrier((value, *others))[0]


def body(sizes, cotangent, saved_panels, upstream, inverse_diag, panel_tops):
    rows, cols = sizes["row"], sizes["col"]
    panels, height, width = saved_panels.shape
    limit = pltpu.CompilerParams(vmem_limit_bytes=32 * 1024 * 1024)
    tile_shape = jax.ShapeDtypeStruct(saved_panels.shape, BF16)

    far = {bits: swap(saved_panels, ("row",), sizes, {"row": bits}) for bits in range(rows - 2, 0, -2)}
    near = {1: swap(saved_panels, ("row",), sizes, {"row": 1})}
    along_col = [(0,)]
    col_tiles = [saved_panels]
    for power in range(cols.bit_length() - 1):
        have = [bits for group in along_col for bits in group]
        sent = jnp.concatenate([tile.reshape(-1, panels, height, width) for tile in col_tiles])
        along_col.append(tuple(bits ^ (1 << power) for bits in have))
        col_tiles.append(swap(sent, ("col",), sizes, {"col": 1 << power}))

    groups = [[2], [bits for bits in far if bits != 2]]
    along_row = [(0,), (1,)]
    row_tiles = [None, near[1][None]]
    for group in groups:
        if not group or group[0] not in far:
            continue
        sent = after(jnp.stack([far[bits] for bits in group]), near[1])
        for bits in group:
            along_row.append((bits,))
            row_tiles.append(far[bits][None])
        along_row.append(tuple(bits ^ 1 for bits in group))
        row_tiles.append(swap(sent, ("row",), sizes, {"row": 1}))

    cot, saved, upstream_here, high, low = pl.pallas_call(
        prepare_kernel,
        out_shape=[
            jax.ShapeDtypeStruct(cotangent.shape, BF16),
            tile_shape,
            tile_shape,
            jax.ShapeDtypeStruct(inverse_diag.shape, BF16),
            jax.ShapeDtypeStruct(inverse_diag.shape, BF16),
        ],
        in_specs=[VMEM] * 4,
        out_specs=[VMEM] * 5,
        compiler_params=limit,
    )(cotangent, saved_panels, upstream, inverse_diag)
    row_tiles[0] = saved[None]
    col_tiles[0] = saved[None]

    piece = panels * width // 8
    columns_keep, columns_send, keep, send = pl.pallas_call(
        functools.partial(main_kernel, along_row, along_col),
        out_shape=[
            jax.ShapeDtypeStruct((cols // 2, panels, height, width), F32),
            jax.ShapeDtypeStruct((cols // 2, panels, height, width), BF16),
            jax.ShapeDtypeStruct((4, piece, width), F32),
            jax.ShapeDtypeStruct((4, piece, width), BF16),
        ],
        in_specs=[VMEM] * (len(row_tiles) + len(col_tiles) + 5),
        out_specs=[VMEM] * 4,
        scratch_shapes=[
            pltpu.VMEM((rows * height, panels * width), BF16),
            pltpu.VMEM((cols * height, panels * width), BF16),
            pltpu.VMEM((cols * height, panels * width), F32),
            pltpu.VMEM((panels * width, width), F32),
        ],
        compiler_params=limit,
    )(*row_tiles, *col_tiles, cot, upstream_here, high, low, panel_tops)

    both = ("row", "col")
    half = keep + swap(send, ("col",), sizes, {"col": 1}).astype(F32)
    spots = [{"col": (bits >> 1) * 2, "row": bits & 1} for bits in range(4)]
    total = half[0]
    for bits in range(3, 0, -1):
        total = total + swap(half[bits].astype(BF16), both, sizes, spots[bits]).astype(F32)
    columns = columns_keep + swap(after(columns_send, half), ("col",), sizes, {"col": 1}).astype(F32)
    held = total
    for power in range(1, cols.bit_length() - 1):
        halves = columns.reshape(-1, 2, panels, height, width)
        sent = after(halves[:, 1].astype(BF16), held)
        columns = halves[:, 0] + swap(sent, ("col",), sizes, {"col": 1 << power}).astype(F32)
    columns = columns[0].astype(BF16)

    others = [{"row": 1 << power} for power in range(1, rows.bit_length() - 1)]
    others += [{"col": 1 << power} for power in range(2, cols.bit_length() - 1)]
    if len(others) == 2 and "col" not in others[1]:
        mine = total.astype(BF16)
        first, second = others[0]["row"], others[1]["row"]
        from_both, from_second, from_first = [
            swap(mine, ("row",), sizes, {"row": bits}) for bits in (first ^ second, second, first)
        ]
        total = (mine.astype(F32) + from_first.astype(F32)) + (
            from_second.astype(F32) + from_both.astype(F32)
        )
    else:
        for bits in others:
            mine = total.astype(BF16)
            total = mine.astype(F32) + swap(mine, tuple(bits), sizes, bits).astype(F32)
    mine = total.astype(BF16)
    here = jnp.stack([mine] + [swap(mine, both, sizes, spots[bits]) for bits in range(3, 0, -1)][::-1])
    there = swap(here, ("col",), sizes, {"col": 1})
    diag_cot = pl.pallas_call(
        finish_kernel,
        out_shape=jax.ShapeDtypeStruct((panels * width, width), F32),
        in_specs=[VMEM] * 2,
        out_specs=VMEM,
        compiler_params=limit,
    )(here, there)
    return columns, diag_cot.reshape(panels, width, width)


def solution(mesh):
    in_specs = (
        P("row", "col"),
        P(None, ("row", "col"), None),
        P(None, ("row", "col"), None),
        P(),
        P(),
    )
    out_specs = (P(None, ("row", "col"), None), P())
    return jax.shard_map(
        functools.partial(body, dict(mesh.shape)),
        mesh=mesh,
        in_specs=in_specs,
        out_specs=out_specs,
        check_vma=False,
    )
```

```python
import functools

import jax
import jax.numpy as jnp
from jax import lax
from jax.experimental import pallas as pl
from jax.experimental.pallas import tpu as pltpu
from jax.sharding import PartitionSpec as P

F32 = jnp.float32
BF16 = jnp.bfloat16
VMEM = pl.BlockSpec(memory_space=pltpu.VMEM)


def swap(value, axes, sizes, bits):
    dims = [sizes[axis] for axis in axes]
    pairs = []
    count = 1
    for dim in dims:
        count *= dim
    for source in range(count):
        rest, coords = source, []
        for dim in reversed(dims):
            coords.append(rest % dim)
            rest //= dim
        coords = coords[::-1]
        target = 0
        for axis, dim, coord in zip(axes, dims, coords):
            target = target * dim + (coord ^ bits.get(axis, 0))
        pairs.append((source, target))
    return lax.ppermute(value, axes, pairs)


def split(value):
    high = value.astype(BF16)
    return high, (value - high.astype(F32)).astype(BF16)


def dot(left, right):
    return jnp.dot(left, right, preferred_element_type=F32)


def dot_rows(left, right):
    return lax.dot_general(left, right, (((0,), (0,)), ((), ())), preferred_element_type=F32)


def prepare_kernel(*refs):
    sources, outs, (high_out, low_out, solver, sems) = refs[:5], refs[5:9], refs[9:]
    copies = [
        pltpu.make_async_copy(source, target, sems.at[index])
        for index, (source, target) in enumerate(zip(sources, (solver, *outs)))
    ]
    for copy in copies:
        copy.start()
    copies[0].wait()
    high, low = split(solver[...])
    high_out[...] = high
    low_out[...] = low
    for copy in copies[1:]:
        copy.wait()


def main_kernel(along_row, along_col, *refs):
    row_refs, refs = refs[: len(along_row)], refs[len(along_row) :]
    col_refs, refs = refs[: len(along_col)], refs[len(along_col) :]
    cot_ref, upstream_ref, high_ref, low_ref, tops_ref = refs[:5]
    columns_keep, columns_send, keep_ref, send_ref, joined, own, total, diag = refs[5:]
    row, col = lax.axis_index("row"), lax.axis_index("col")
    panels, height, width = upstream_ref.shape

    def place(target, index, tile):
        start = pl.multiple_of(index * height, height)
        for panel in range(panels):
            target[pl.ds(start, height), panel * width : (panel + 1) * width] = tile[panel]

    for bits_list, ref in zip(along_row, row_refs):
        for spot, bits in enumerate(bits_list):
            place(joined, row ^ bits, ref.at[spot])
    for bits_list, ref in zip(along_col, col_refs):
        for spot, bits in enumerate(bits_list):
            place(own, col ^ bits, ref.at[spot])
    total[...] = -2.0 * dot(cot_ref[...], joined[...])
    mine = pl.ds(pl.multiple_of(col * height, height), height)
    for index in range(panels):
        span = slice(index * width, (index + 1) * width)
        total[mine, span] += upstream_ref[index].astype(F32)

    columns = []
    tall = own.shape[0]
    for index in range(panels):
        span = slice(index * width, (index + 1) * width)
        panel = own[:, span]
        combined = total[:, span]
        appended = None
        for earlier in range(index):
            term = dot(columns[earlier], tops_ref[index * (index - 1) // 2 + earlier])
            appended = term if appended is None else appended + term
        if appended is not None:
            combined = combined - 2.0 * appended
        high, low = split(combined)
        if appended is None:
            first = dot(jnp.concatenate([high, low]), high_ref[index])
            second = dot(high, low_ref[index])
        else:
            first = dot(jnp.concatenate([high, low, panel]), high_ref[index])
            second = dot(jnp.concatenate([high, panel]), low_ref[index])
        now = first[:tall] + (first[tall : 2 * tall] + second[:tall])
        total[:, span] = now
        now = now.astype(BF16)
        columns.append(now)
        result = -dot_rows(panel, now)
        if appended is not None:
            solved = 2.0 * (first[2 * tall :] + second[tall:])
            result = result + dot_rows(appended.astype(BF16), solved.astype(BF16))
        diag[span, :] = result

    piece = keep_ref.shape[1]
    core, spot = place_of()
    for bits in range(4):
        here = pl.multiple_of((core * 4 + (spot ^ bits)) * piece, piece)
        there = pl.multiple_of(((1 - core) * 4 + (spot ^ bits)) * piece, piece)
        keep_ref[bits] = diag[pl.ds(here, piece), :]
        send_ref[bits] = diag[pl.ds(there, piece), :].astype(BF16)
    for pair in range(columns_keep.shape[0]):
        for bits, ref in ((2 * pair, columns_keep), (2 * pair + 1, columns_send)):
            tile = pl.ds(pl.multiple_of((col ^ bits) * height, height), height)
            for index in range(panels):
                ref[pair, index] = total[tile, index * width : (index + 1) * width].astype(ref.dtype)


def place_of():
    row, col = lax.axis_index("row"), lax.axis_index("col")
    return col & 1, ((col >> 1) & 1) * 2 + (row & 1)


def finish_kernel(here_ref, there_ref, out_ref):
    core, spot = place_of()
    piece = here_ref.shape[1]
    for bits in range(4):
        here = pl.multiple_of((core * 4 + (spot ^ bits)) * piece, piece)
        there = pl.multiple_of(((1 - core) * 4 + (spot ^ bits)) * piece, piece)
        out_ref[pl.ds(here, piece), :] = here_ref[bits].astype(F32)
        out_ref[pl.ds(there, piece), :] = there_ref[bits].astype(F32)


def after(value, *others):
    return lax.optimization_barrier((value, *others))[0]


def body(sizes, cotangent, saved_panels, upstream, inverse_diag, panel_tops):
    rows, cols = sizes["row"], sizes["col"]
    panels, height, width = saved_panels.shape
    limit = pltpu.CompilerParams(vmem_limit_bytes=32 * 1024 * 1024)
    tile_shape = jax.ShapeDtypeStruct(saved_panels.shape, BF16)

    near = [bits for bits in (1, 2, 3) if bits < rows]
    along_row, row_tiles = [(0,)], [None]
    far = [bits for bits in range(4, rows, 4)]
    crossed = [swap(saved_panels, ("row",), sizes, {"row": bits}) for bits in far]
    nearby = {bits: swap(saved_panels, ("row",), sizes, {"row": bits}) for bits in near}
    along_col = [(0,)]
    col_tiles = [None]
    for power in list(range(1, cols.bit_length() - 1)) + [0]:
        held = [(bits, tile) for (bits,), tile in zip(along_col, col_tiles)]
        for bits, tile in held:
            along_col.append((bits ^ (1 << power),))
            sent = saved_panels if tile is None else tile[0]
            col_tiles.append(swap(sent, ("col",), sizes, {"col": 1 << power})[None])
    for bits in near:
        along_row.append((bits,))
        row_tiles.append(nearby[bits][None])
    if far:
        sent = jnp.stack(crossed)
        along_row.append(tuple(far))
        row_tiles.append(sent)
        for bits in near:
            along_row.append(tuple(other ^ bits for other in far))
            row_tiles.append(swap(sent, ("row",), sizes, {"row": bits}))

    arguments = (inverse_diag, cotangent, saved_panels, upstream, panel_tops)
    halves = [jax.ShapeDtypeStruct(inverse_diag.shape, BF16)] * 2
    cot, saved, upstream_here, tops, high, low = pl.pallas_call(
        prepare_kernel,
        out_shape=[jax.ShapeDtypeStruct(value.shape, BF16) for value in arguments[1:]] + halves,
        in_specs=[pl.BlockSpec(memory_space=pl.ANY)] * 5,
        out_specs=[VMEM] * 6,
        scratch_shapes=[pltpu.VMEM(inverse_diag.shape, F32), pltpu.SemaphoreType.DMA((5,))],
        compiler_params=limit,
    )(*[pltpu.with_memory_space_constraint(value, pltpu.HBM) for value in arguments])
    row_tiles[0] = saved[None]
    col_tiles[0] = saved[None]

    piece = panels * width // 8
    columns_keep, columns_send, keep, send = pl.pallas_call(
        functools.partial(main_kernel, along_row, along_col),
        out_shape=[
            jax.ShapeDtypeStruct((cols // 2, panels, height, width), F32),
            jax.ShapeDtypeStruct((cols // 2, panels, height, width), BF16),
            jax.ShapeDtypeStruct((4, piece, width), F32),
            jax.ShapeDtypeStruct((4, piece, width), BF16),
        ],
        in_specs=[VMEM] * (len(row_tiles) + len(col_tiles) + 5),
        out_specs=[VMEM] * 4,
        scratch_shapes=[
            pltpu.VMEM((rows * height, panels * width), BF16),
            pltpu.VMEM((cols * height, panels * width), BF16),
            pltpu.VMEM((cols * height, panels * width), F32),
            pltpu.VMEM((panels * width, width), F32),
        ],
        compiler_params=limit,
    )(*row_tiles, *col_tiles, cot, upstream_here, high, low, tops)

    both = ("row", "col")
    half = keep + swap(send, ("col",), sizes, {"col": 1}).astype(F32)
    spots = [{"col": (bits >> 1) * 2, "row": bits & 1} for bits in range(4)]
    total = half[0]
    for bits in range(3, 0, -1):
        total = total + swap(half[bits].astype(BF16), both, sizes, spots[bits]).astype(F32)
    arrived = swap(after(columns_send, half), ("col",), sizes, {"col": 1})
    columns = columns_keep + arrived.astype(F32)
    mine = after(total.astype(BF16), arrived)
    for power in range(1, cols.bit_length() - 1):
        halves = columns.reshape(-1, 2, panels, height, width)
        arrived = swap(after(halves[:, 1].astype(BF16), mine), ("col",), sizes, {"col": 1 << power})
        columns = halves[:, 0] + arrived.astype(F32)
    columns = columns[0].astype(BF16)

    others = [{"row": 1 << power} for power in range(1, rows.bit_length() - 1)]
    others += [{"col": 1 << power} for power in range(2, cols.bit_length() - 1)]
    if len(others) == 2 and "col" not in others[1]:
        first, second = others[0]["row"], others[1]["row"]
        from_first, from_second, from_both = [
            swap(mine, ("row",), sizes, {"row": bits}) for bits in (first, second, first ^ second)
        ]
        total = (mine.astype(F32) + from_first.astype(F32)) + (
            from_second.astype(F32) + from_both.astype(F32)
        )
    else:
        for bits in others:
            total = mine.astype(F32) + swap(mine, tuple(bits), sizes, bits).astype(F32)
            mine = total.astype(BF16)
    mine = after(total.astype(BF16), arrived)
    here = jnp.stack([mine] + [swap(mine, both, sizes, spots[bits]) for bits in range(1, 4)])
    there = swap(here, ("col",), sizes, {"col": 1})
    diag_cot = pl.pallas_call(
        finish_kernel,
        out_shape=jax.ShapeDtypeStruct((panels * width, width), F32),
        in_specs=[VMEM] * 2,
        out_specs=VMEM,
        compiler_params=limit,
    )(here, there)
    return columns, diag_cot.reshape(panels, width, width)


def solution(mesh):
    in_specs = (
        P("row", "col"),
        P(None, ("row", "col"), None),
        P(None, ("row", "col"), None),
        P(),
        P(),
    )
    out_specs = (P(None, ("row", "col"), None), P())
    return jax.shard_map(
        functools.partial(body, dict(mesh.shape)),
        mesh=mesh,
        in_specs=in_specs,
        out_specs=out_specs,
        check_vma=False,
    )
```

```python
import functools

import jax
import jax.numpy as jnp
from jax import lax
from jax.experimental import pallas as pl
from jax.experimental.pallas import tpu as pltpu
from jax.sharding import PartitionSpec as P

F32 = jnp.float32
BF16 = jnp.bfloat16
VMEM = pl.BlockSpec(memory_space=pltpu.VMEM)


def swap(value, axes, sizes, bits):
    dims = [sizes[axis] for axis in axes]
    pairs = []
    count = 1
    for dim in dims:
        count *= dim
    for source in range(count):
        rest, coords = source, []
        for dim in reversed(dims):
            coords.append(rest % dim)
            rest //= dim
        coords = coords[::-1]
        target = 0
        for axis, dim, coord in zip(axes, dims, coords):
            target = target * dim + (coord ^ bits.get(axis, 0))
        pairs.append((source, target))
    return lax.ppermute(value, axes, pairs)


def split(value):
    high = value.astype(BF16)
    return high, (value - high.astype(F32)).astype(BF16)


def dot(left, right):
    return jnp.dot(left, right, preferred_element_type=F32)


def dot_rows(left, right):
    return lax.dot_general(left, right, (((0,), (0,)), ((), ())), preferred_element_type=F32)


def prepare_kernel(*refs):
    sources, outs, (high_out, low_out, solver, sems) = refs[:5], refs[5:9], refs[9:]
    copies = [
        pltpu.make_async_copy(source, target, sems.at[index])
        for index, (source, target) in enumerate(zip(sources, (solver, *outs)))
    ]
    for copy in copies:
        copy.start()
    copies[0].wait()
    high, low = split(solver[...])
    high_out[...] = high
    low_out[...] = low
    for copy in copies[1:]:
        copy.wait()


def main_kernel(along_row, along_col, *refs):
    row_refs, refs = refs[: len(along_row)], refs[len(along_row) :]
    col_refs, refs = refs[: len(along_col)], refs[len(along_col) :]
    cot_ref, upstream_ref, high_ref, low_ref, tops_ref = refs[:5]
    columns_keep, columns_send, keep_ref, send_ref, joined, own, total, diag = refs[5:]
    row, col = lax.axis_index("row"), lax.axis_index("col")
    panels, height, width = upstream_ref.shape

    def place(target, index, tile):
        start = pl.multiple_of(index * height, height)
        for panel in range(panels):
            target[pl.ds(start, height), panel * width : (panel + 1) * width] = tile[panel]

    for bits_list, ref in zip(along_row, row_refs):
        for spot, bits in enumerate(bits_list):
            place(joined, row ^ bits, ref.at[spot])
    for bits_list, ref in zip(along_col, col_refs):
        for spot, bits in enumerate(bits_list):
            place(own, col ^ bits, ref.at[spot])
    total[...] = -2.0 * dot(cot_ref[...], joined[...])
    mine = pl.ds(pl.multiple_of(col * height, height), height)
    for index in range(panels):
        span = slice(index * width, (index + 1) * width)
        total[mine, span] += upstream_ref[index].astype(F32)

    columns = []
    tall = own.shape[0]
    for index in range(panels):
        span = slice(index * width, (index + 1) * width)
        panel = own[:, span]
        combined = total[:, span]
        appended = None
        for earlier in range(index):
            term = dot(columns[earlier], tops_ref[index * (index - 1) // 2 + earlier])
            appended = term if appended is None else appended + term
        if appended is not None:
            combined = combined - 2.0 * appended
        high, low = split(combined)
        if appended is None:
            first = dot(jnp.concatenate([high, low]), high_ref[index])
            second = dot(high, low_ref[index])
        else:
            first = dot(jnp.concatenate([high, low, panel]), high_ref[index])
            second = dot(jnp.concatenate([high, panel]), low_ref[index])
        now = first[:tall] + (first[tall : 2 * tall] + second[:tall])
        total[:, span] = now
        now = now.astype(BF16)
        columns.append(now)
        result = -dot_rows(panel, now)
        if appended is not None:
            solved = 2.0 * (first[2 * tall :] + second[tall:])
            result = result + dot_rows(appended.astype(BF16), solved.astype(BF16))
        diag[span, :] = result

    piece = keep_ref.shape[1]
    core, spot = place_of()
    for bits in range(4):
        here = pl.multiple_of((core * 4 + (spot ^ bits)) * piece, piece)
        there = pl.multiple_of(((1 - core) * 4 + (spot ^ bits)) * piece, piece)
        keep_ref[bits] = diag[pl.ds(here, piece), :]
        send_ref[bits] = diag[pl.ds(there, piece), :].astype(BF16)
    for pair in range(columns_keep.shape[0]):
        for bits, ref in ((2 * pair, columns_keep), (2 * pair + 1, columns_send)):
            tile = pl.ds(pl.multiple_of((col ^ bits) * height, height), height)
            for index in range(panels):
                ref[pair, index] = total[tile, index * width : (index + 1) * width].astype(ref.dtype)


def place_of():
    row, col = lax.axis_index("row"), lax.axis_index("col")
    return col & 1, ((col >> 1) & 1) * 2 + (row & 1)


def finish_kernel(here_ref, there_ref, out_ref):
    core, spot = place_of()
    piece = here_ref.shape[1]
    for bits in range(4):
        here = pl.multiple_of((core * 4 + (spot ^ bits)) * piece, piece)
        there = pl.multiple_of(((1 - core) * 4 + (spot ^ bits)) * piece, piece)
        out_ref[pl.ds(here, piece), :] = here_ref[bits].astype(F32)
        out_ref[pl.ds(there, piece), :] = there_ref[bits].astype(F32)


def after(value, *others):
    return lax.optimization_barrier((value, *others))[0]


def body(sizes, cotangent, saved_panels, upstream, inverse_diag, panel_tops):
    rows, cols = sizes["row"], sizes["col"]
    panels, height, width = saved_panels.shape
    limit = pltpu.CompilerParams(vmem_limit_bytes=32 * 1024 * 1024)
    tile_shape = jax.ShapeDtypeStruct(saved_panels.shape, BF16)

    near = [bits for bits in (1, 2, 3) if bits < rows]
    along_row, row_tiles = [(0,)], [None]
    far = [bits for bits in range(4, rows, 4)]
    crossed = [swap(saved_panels, ("row",), sizes, {"row": bits}) for bits in far]
    nearby = {bits: swap(saved_panels, ("row",), sizes, {"row": bits}) for bits in near}
    along_col = [(0,)]
    col_tiles = [None]
    for power in list(range(1, cols.bit_length() - 1)) + [0]:
        held = [(bits, tile) for (bits,), tile in zip(along_col, col_tiles)]
        for bits, tile in held:
            along_col.append((bits ^ (1 << power),))
            sent = saved_panels if tile is None else tile[0]
            if power == 0 and tile is None and len(held) > 1:
                sent = after(sent, held[-1][1])
            col_tiles.append(swap(sent, ("col",), sizes, {"col": 1 << power})[None])
    for bits in near:
        along_row.append((bits,))
        row_tiles.append(nearby[bits][None])
    if far:
        sent = jnp.stack(crossed)
        along_row.append(tuple(far))
        row_tiles.append(sent)
        for bits in near:
            along_row.append(tuple(other ^ bits for other in far))
            row_tiles.append(swap(sent, ("row",), sizes, {"row": bits}))

    arguments = (inverse_diag, cotangent, saved_panels, upstream, panel_tops)
    halves = [jax.ShapeDtypeStruct(inverse_diag.shape, BF16)] * 2
    cot, saved, upstream_here, tops, high, low = pl.pallas_call(
        prepare_kernel,
        out_shape=[jax.ShapeDtypeStruct(value.shape, BF16) for value in arguments[1:]] + halves,
        in_specs=[pl.BlockSpec(memory_space=pl.ANY)] * 5,
        out_specs=[VMEM] * 6,
        scratch_shapes=[pltpu.VMEM(inverse_diag.shape, F32), pltpu.SemaphoreType.DMA((5,))],
        compiler_params=limit,
    )(*[pltpu.with_memory_space_constraint(value, pltpu.HBM) for value in arguments])
    row_tiles[0] = saved[None]
    col_tiles[0] = saved[None]

    piece = panels * width // 8
    columns_keep, columns_send, keep, send = pl.pallas_call(
        functools.partial(main_kernel, along_row, along_col),
        out_shape=[
            jax.ShapeDtypeStruct((cols // 2, panels, height, width), F32),
            jax.ShapeDtypeStruct((cols // 2, panels, height, width), BF16),
            jax.ShapeDtypeStruct((4, piece, width), F32),
            jax.ShapeDtypeStruct((4, piece, width), BF16),
        ],
        in_specs=[VMEM] * (len(row_tiles) + len(col_tiles) + 5),
        out_specs=[VMEM] * 4,
        scratch_shapes=[
            pltpu.VMEM((rows * height, panels * width), BF16),
            pltpu.VMEM((cols * height, panels * width), BF16),
            pltpu.VMEM((cols * height, panels * width), F32),
            pltpu.VMEM((panels * width, width), F32),
        ],
        compiler_params=limit,
    )(*row_tiles, *col_tiles, cot, upstream_here, high, low, tops)

    both = ("row", "col")
    half = keep + swap(send, ("col",), sizes, {"col": 1}).astype(F32)
    spots = [{"col": (bits >> 1) * 2, "row": bits & 1} for bits in range(4)]
    total = half[0]
    for bits in range(3, 0, -1):
        total = total + swap(half[bits].astype(BF16), both, sizes, spots[bits]).astype(F32)
    arrived = swap(after(columns_send, half), ("col",), sizes, {"col": 1})
    columns = columns_keep + arrived.astype(F32)
    mine = after(total.astype(BF16), arrived)
    for power in range(1, cols.bit_length() - 1):
        halves = columns.reshape(-1, 2, panels, height, width)
        arrived = swap(after(halves[:, 1].astype(BF16), mine), ("col",), sizes, {"col": 1 << power})
        columns = halves[:, 0] + arrived.astype(F32)
    columns = columns[0].astype(BF16)

    others = [{"row": 1 << power} for power in range(1, rows.bit_length() - 1)]
    others += [{"col": 1 << power} for power in range(2, cols.bit_length() - 1)]
    if len(others) == 2 and "col" not in others[1]:
        first, second = others[0]["row"], others[1]["row"]
        from_first, from_second, from_both = [
            swap(mine, ("row",), sizes, {"row": bits}) for bits in (first, second, first ^ second)
        ]
        from_second, from_first, from_both, arrived = lax.optimization_barrier(
            (from_second, from_first, from_both, arrived)
        )
        total = (mine.astype(F32) + from_first.astype(F32)) + (
            from_second.astype(F32) + from_both.astype(F32)
        )
    else:
        for bits in others:
            total = mine.astype(F32) + swap(mine, tuple(bits), sizes, bits).astype(F32)
            mine = total.astype(BF16)
    mine = total.astype(BF16)
    here = jnp.stack([mine] + [swap(mine, both, sizes, spots[bits]) for bits in range(1, 4)])
    there = swap(here, ("col",), sizes, {"col": 1})
    diag_cot = pl.pallas_call(
        finish_kernel,
        out_shape=jax.ShapeDtypeStruct((panels * width, width), F32),
        in_specs=[VMEM] * 2,
        out_specs=VMEM,
        compiler_params=limit,
    )(here, there)
    return columns, diag_cot.reshape(panels, width, width)


def solution(mesh):
    in_specs = (
        P("row", "col"),
        P(None, ("row", "col"), None),
        P(None, ("row", "col"), None),
        P(),
        P(),
    )
    out_specs = (P(None, ("row", "col"), None), P())
    return jax.shard_map(
        functools.partial(body, dict(mesh.shape)),
        mesh=mesh,
        in_specs=in_specs,
        out_specs=out_specs,
        check_vma=False,
    )
```

```python
import functools

import jax
import jax.numpy as jnp
from jax import lax
from jax.experimental import pallas as pl
from jax.experimental.pallas import tpu as pltpu
from jax.sharding import PartitionSpec as P

F32 = jnp.float32
BF16 = jnp.bfloat16
VMEM = pl.BlockSpec(memory_space=pltpu.VMEM)


def swap(value, axes, sizes, bits):
    dims = [sizes[axis] for axis in axes]
    pairs = []
    count = 1
    for dim in dims:
        count *= dim
    for source in range(count):
        rest, coords = source, []
        for dim in reversed(dims):
            coords.append(rest % dim)
            rest //= dim
        coords = coords[::-1]
        target = 0
        for axis, dim, coord in zip(axes, dims, coords):
            target = target * dim + (coord ^ bits.get(axis, 0))
        pairs.append((source, target))
    return lax.ppermute(value, axes, pairs)


def dot(left, right):
    return jnp.dot(left, right, preferred_element_type=F32)


def dot_rows(left, right):
    return lax.dot_general(left, right, (((0,), (0,)), ((), ())), preferred_element_type=F32)


def prepare_kernel(*refs):
    sources, outs, (solver_out, solver, sems) = refs[:5], refs[5:9], refs[9:]
    copies = [
        pltpu.make_async_copy(source, target, sems.at[index])
        for index, (source, target) in enumerate(zip(sources, (solver, *outs)))
    ]
    for copy in copies:
        copy.start()
    copies[0].wait()
    solver_out[...] = solver[...].astype(BF16)
    for copy in copies[1:]:
        copy.wait()


def main_kernel(along_row, along_col, *refs):
    row_refs, refs = refs[: len(along_row)], refs[len(along_row) :]
    col_refs, refs = refs[: len(along_col)], refs[len(along_col) :]
    cot_ref, upstream_ref, solver_ref, tops_ref = refs[:4]
    columns_keep, columns_send, keep_ref, send_ref, joined, own, total, diag = refs[4:]
    row, col = lax.axis_index("row"), lax.axis_index("col")
    panels, height, width = upstream_ref.shape

    def place(target, index, tile):
        start = pl.multiple_of(index * height, height)
        for panel in range(panels):
            target[pl.ds(start, height), panel * width : (panel + 1) * width] = tile[panel]

    for bits_list, ref in zip(along_row, row_refs):
        for spot, bits in enumerate(bits_list):
            place(joined, row ^ bits, ref.at[spot])
    for bits_list, ref in zip(along_col, col_refs):
        for spot, bits in enumerate(bits_list):
            place(own, col ^ bits, ref.at[spot])
    total[...] = -2.0 * dot(cot_ref[...], joined[...])
    mine = pl.ds(pl.multiple_of(col * height, height), height)
    for index in range(panels):
        span = slice(index * width, (index + 1) * width)
        total[mine, span] += upstream_ref[index].astype(F32)

    columns = []
    tall = own.shape[0]
    for index in range(panels):
        span = slice(index * width, (index + 1) * width)
        panel = own[:, span]
        combined = total[:, span]
        appended = None
        for earlier in range(index):
            term = dot(columns[earlier], tops_ref[index * (index - 1) // 2 + earlier])
            appended = term if appended is None else appended + term
        if appended is not None:
            combined = combined - 2.0 * appended
        combined = combined.astype(BF16)
        if appended is None:
            now = dot(combined, solver_ref[index])
        else:
            solved = dot(jnp.concatenate([combined, panel]), solver_ref[index])
            now, solved = solved[:tall], 2.0 * solved[tall:]
        total[:, span] = now
        now = now.astype(BF16)
        columns.append(now)
        if appended is None:
            result = dot_rows(panel, -now)
        else:
            result = dot_rows(
                jnp.concatenate([panel, appended.astype(BF16)]),
                jnp.concatenate([-now, solved.astype(BF16)]),
            )
        diag[span, :] = result

    piece = keep_ref.shape[1]
    core, spot = place_of()
    for bits in range(4):
        here = pl.multiple_of((core * 4 + (spot ^ bits)) * piece, piece)
        there = pl.multiple_of(((1 - core) * 4 + (spot ^ bits)) * piece, piece)
        keep_ref[bits] = diag[pl.ds(here, piece), :]
        send_ref[bits] = diag[pl.ds(there, piece), :].astype(BF16)
    for pair in range(columns_keep.shape[0]):
        for bits, ref in ((2 * pair, columns_keep), (2 * pair + 1, columns_send)):
            tile = pl.ds(pl.multiple_of((col ^ bits) * height, height), height)
            for index in range(panels):
                ref[pair, index] = total[tile, index * width : (index + 1) * width].astype(ref.dtype)


def place_of():
    row, col = lax.axis_index("row"), lax.axis_index("col")
    return col & 1, ((col >> 1) & 1) * 2 + (row & 1)


def finish_kernel(here_ref, there_ref, out_ref):
    core, spot = place_of()
    piece = here_ref.shape[1]
    for bits in range(4):
        here = pl.multiple_of((core * 4 + (spot ^ bits)) * piece, piece)
        there = pl.multiple_of(((1 - core) * 4 + (spot ^ bits)) * piece, piece)
        out_ref[pl.ds(here, piece), :] = here_ref[bits].astype(F32)
        out_ref[pl.ds(there, piece), :] = there_ref[bits].astype(F32)


def after(value, *others):
    return lax.optimization_barrier((value, *others))[0]


def body(sizes, cotangent, saved_panels, upstream, inverse_diag, panel_tops):
    rows, cols = sizes["row"], sizes["col"]
    panels, height, width = saved_panels.shape
    limit = pltpu.CompilerParams(vmem_limit_bytes=32 * 1024 * 1024)
    tile_shape = jax.ShapeDtypeStruct(saved_panels.shape, BF16)

    near = [bits for bits in (1, 2, 3) if bits < rows]
    along_row, row_tiles = [(0,)], [None]
    far = [bits for bits in range(4, rows, 4)]
    crossed = [swap(saved_panels, ("row",), sizes, {"row": bits}) for bits in far]
    nearby = {bits: swap(saved_panels, ("row",), sizes, {"row": bits}) for bits in near}
    along_col = [(0,)]
    col_tiles = [None]
    for power in list(range(1, cols.bit_length() - 1)) + [0]:
        held = [(bits, tile) for (bits,), tile in zip(along_col, col_tiles)]
        for bits, tile in held:
            along_col.append((bits ^ (1 << power),))
            sent = saved_panels if tile is None else tile[0]
            if power == 0 and tile is None and len(held) > 1:
                sent = after(sent, held[-1][1])
            col_tiles.append(swap(sent, ("col",), sizes, {"col": 1 << power})[None])
    for bits in near:
        along_row.append((bits,))
        row_tiles.append(nearby[bits][None])
    if far:
        sent = jnp.stack(crossed)
        along_row.append(tuple(far))
        row_tiles.append(sent)
        for bits in near:
            along_row.append(tuple(other ^ bits for other in far))
            row_tiles.append(swap(sent, ("row",), sizes, {"row": bits}))

    arguments = (inverse_diag, cotangent, saved_panels, upstream, panel_tops)
    cot, saved, upstream_here, tops, solver = pl.pallas_call(
        prepare_kernel,
        out_shape=[jax.ShapeDtypeStruct(value.shape, BF16) for value in arguments[1:] + arguments[:1]],
        in_specs=[pl.BlockSpec(memory_space=pl.ANY)] * 5,
        out_specs=[VMEM] * 5,
        scratch_shapes=[pltpu.VMEM(inverse_diag.shape, F32), pltpu.SemaphoreType.DMA((5,))],
        compiler_params=limit,
    )(*[pltpu.with_memory_space_constraint(value, pltpu.HBM) for value in arguments])
    row_tiles[0] = saved[None]
    col_tiles[0] = saved[None]

    piece = panels * width // 8
    columns_keep, columns_send, keep, send = pl.pallas_call(
        functools.partial(main_kernel, along_row, along_col),
        out_shape=[
            jax.ShapeDtypeStruct((cols // 2, panels, height, width), F32),
            jax.ShapeDtypeStruct((cols // 2, panels, height, width), BF16),
            jax.ShapeDtypeStruct((4, piece, width), F32),
            jax.ShapeDtypeStruct((4, piece, width), BF16),
        ],
        in_specs=[VMEM] * (len(row_tiles) + len(col_tiles) + 4),
        out_specs=[VMEM] * 4,
        scratch_shapes=[
            pltpu.VMEM((rows * height, panels * width), BF16),
            pltpu.VMEM((cols * height, panels * width), BF16),
            pltpu.VMEM((cols * height, panels * width), F32),
            pltpu.VMEM((panels * width, width), F32),
        ],
        compiler_params=limit,
    )(*row_tiles, *col_tiles, cot, upstream_here, solver, tops)

    both = ("row", "col")
    half = keep + swap(send, ("col",), sizes, {"col": 1}).astype(F32)
    spots = [{"col": (bits >> 1) * 2, "row": bits & 1} for bits in range(4)]
    total = half[0]
    for bits in (3, 1, 2):
        total = total + swap(half[bits].astype(BF16), both, sizes, spots[bits]).astype(F32)
    arrived = swap(columns_send, ("col",), sizes, {"col": 1})
    columns = columns_keep + arrived.astype(F32)
    for power in range(1, cols.bit_length() - 1):
        halves = columns.reshape(-1, 2, panels, height, width)
        arrived = swap(after(halves[:, 1].astype(BF16), half), ("col",), sizes, {"col": 1 << power})
        columns = halves[:, 0] + arrived.astype(F32)
    mine = total.astype(BF16)
    columns = columns[0].astype(BF16)

    others = [{"row": 1 << power} for power in range(1, rows.bit_length() - 1)]
    others += [{"col": 1 << power} for power in range(2, cols.bit_length() - 1)]
    if len(others) == 2 and "col" not in others[1]:
        first, second = others[0]["row"], others[1]["row"]
        from_first, from_second, from_both = [
            swap(mine, ("row",), sizes, {"row": bits}) for bits in (first, second, first ^ second)
        ]
        from_second, from_first, from_both, arrived = lax.optimization_barrier(
            (from_second, from_first, from_both, arrived)
        )
        total = (mine.astype(F32) + from_first.astype(F32)) + (
            from_second.astype(F32) + from_both.astype(F32)
        )
    else:
        for bits in others:
            total = mine.astype(F32) + swap(mine, tuple(bits), sizes, bits).astype(F32)
            mine = total.astype(BF16)
    mine = total.astype(BF16)
    here = jnp.stack([mine] + [swap(mine, both, sizes, spots[bits]) for bits in range(1, 4)])
    there = swap(here, ("col",), sizes, {"col": 1})
    diag_cot = pl.pallas_call(
        finish_kernel,
        out_shape=jax.ShapeDtypeStruct((panels * width, width), F32),
        in_specs=[VMEM] * 2,
        out_specs=VMEM,
        compiler_params=limit,
    )(here, there)
    return columns, diag_cot.reshape(panels, width, width)


def solution(mesh):
    in_specs = (
        P("row", "col"),
        P(None, ("row", "col"), None),
        P(None, ("row", "col"), None),
        P(),
        P(),
    )
    out_specs = (P(None, ("row", "col"), None), P())
    return jax.shard_map(
        functools.partial(body, dict(mesh.shape)),
        mesh=mesh,
        in_specs=in_specs,
        out_specs=out_specs,
        check_vma=False,
    )
```

```python
import functools

import jax
import jax.numpy as jnp
from jax import lax
from jax.experimental import pallas as pl
from jax.experimental.pallas import tpu as pltpu
from jax.sharding import PartitionSpec as P

F32 = jnp.float32
BF16 = jnp.bfloat16
VMEM = pl.BlockSpec(memory_space=pltpu.VMEM)


def swap(value, axes, sizes, bits):
    dims = [sizes[axis] for axis in axes]
    pairs = []
    count = 1
    for dim in dims:
        count *= dim
    for source in range(count):
        rest, coords = source, []
        for dim in reversed(dims):
            coords.append(rest % dim)
            rest //= dim
        coords = coords[::-1]
        target = 0
        for axis, dim, coord in zip(axes, dims, coords):
            target = target * dim + (coord ^ bits.get(axis, 0))
        pairs.append((source, target))
    return lax.ppermute(value, axes, pairs)


def dot(left, right):
    return jnp.dot(left, right, preferred_element_type=F32)


def dot_rows(left, right):
    return lax.dot_general(left, right, (((0,), (0,)), ((), ())), preferred_element_type=F32)


def prepare_kernel(*refs):
    sources, outs, (solver_out, solver, sems) = refs[:5], refs[5:9], refs[9:]
    copies = [
        pltpu.make_async_copy(source, target, sems.at[index])
        for index, (source, target) in enumerate(zip(sources, (solver, *outs)))
    ]
    for copy in copies:
        copy.start()
    copies[0].wait()
    solver_out[...] = solver[...].astype(BF16)
    for copy in copies[1:]:
        copy.wait()


def main_kernel(along_row, along_col, *refs):
    row_refs, refs = refs[: len(along_row)], refs[len(along_row) :]
    col_refs, refs = refs[: len(along_col)], refs[len(along_col) :]
    cot_ref, upstream_ref, solver_ref, tops_ref = refs[:4]
    columns_keep, columns_send, keep_ref, send_ref, joined, own, total, diag = refs[4:]
    row, col = lax.axis_index("row"), lax.axis_index("col")
    panels, height, width = upstream_ref.shape

    def place(target, index, tile):
        start = pl.multiple_of(index * height, height)
        for panel in range(panels):
            target[pl.ds(start, height), panel * width : (panel + 1) * width] = tile[panel]

    for bits_list, ref in zip(along_row, row_refs):
        for spot, bits in enumerate(bits_list):
            place(joined, row ^ bits, ref.at[spot])
    for bits_list, ref in zip(along_col, col_refs):
        for spot, bits in enumerate(bits_list):
            place(own, col ^ bits, ref.at[spot])
    total[...] = -2.0 * dot(cot_ref[...], joined[...])
    mine = pl.ds(pl.multiple_of(col * height, height), height)
    for index in range(panels):
        span = slice(index * width, (index + 1) * width)
        total[mine, span] += upstream_ref[index].astype(F32)

    columns = []
    tall = own.shape[0]
    for index in range(panels):
        span = slice(index * width, (index + 1) * width)
        panel = own[:, span]
        combined = total[:, span]
        appended = None
        for earlier in range(index):
            term = dot(columns[earlier], tops_ref[index * (index - 1) // 2 + earlier])
            appended = term if appended is None else appended + term
        if appended is not None:
            combined = combined - 2.0 * appended
        combined = combined.astype(BF16)
        if appended is None:
            now = dot(combined, solver_ref[index])
        else:
            solved = dot(jnp.concatenate([combined, panel]), solver_ref[index])
            now, solved = solved[:tall], 2.0 * solved[tall:]
        total[:, span] = now
        now = now.astype(BF16)
        columns.append(now)
        if appended is None:
            result = dot_rows(panel, -now)
        else:
            result = dot_rows(
                jnp.concatenate([panel, appended.astype(BF16)]),
                jnp.concatenate([-now, solved.astype(BF16)]),
            )
        diag[span, :] = result

    piece = keep_ref.shape[1]
    core, spot = place_of()
    for bits in range(4):
        here = pl.multiple_of((core * 4 + (spot ^ bits)) * piece, piece)
        there = pl.multiple_of(((1 - core) * 4 + (spot ^ bits)) * piece, piece)
        keep_ref[bits] = diag[pl.ds(here, piece), :]
        send_ref[bits] = diag[pl.ds(there, piece), :].astype(BF16)
    for pair in range(columns_keep.shape[0]):
        for bits, ref in ((2 * pair, columns_keep), (2 * pair + 1, columns_send)):
            tile = pl.ds(pl.multiple_of((col ^ bits) * height, height), height)
            for index in range(panels):
                ref[pair, index] = total[tile, index * width : (index + 1) * width].astype(ref.dtype)


def place_of():
    row, col = lax.axis_index("row"), lax.axis_index("col")
    return col & 1, ((col >> 1) & 1) * 2 + (row & 1)


def finish_kernel(here_ref, there_ref, out_ref):
    core, spot = place_of()
    piece = here_ref.shape[1]
    for bits in range(4):
        here = pl.multiple_of((core * 4 + (spot ^ bits)) * piece, piece)
        there = pl.multiple_of(((1 - core) * 4 + (spot ^ bits)) * piece, piece)
        out_ref[pl.ds(here, piece), :] = here_ref[bits].astype(F32)
        out_ref[pl.ds(there, piece), :] = there_ref[bits].astype(F32)


def after(value, *others):
    return lax.optimization_barrier((value, *others))[0]


def body(sizes, cotangent, saved_panels, upstream, inverse_diag, panel_tops):
    rows, cols = sizes["row"], sizes["col"]
    panels, height, width = saved_panels.shape
    limit = pltpu.CompilerParams(vmem_limit_bytes=32 * 1024 * 1024)
    tile_shape = jax.ShapeDtypeStruct(saved_panels.shape, BF16)

    near = [bits for bits in (1, 2, 3) if bits < rows]
    along_row, row_tiles = [(0,)], [None]
    far = [bits for bits in range(4, rows, 4)]
    crossed = [swap(saved_panels, ("row",), sizes, {"row": bits}) for bits in far]
    nearby = {bits: swap(saved_panels, ("row",), sizes, {"row": bits}) for bits in near}
    along_col = [(0,)]
    col_tiles = [None]
    for power in list(range(1, cols.bit_length() - 1)) + [0]:
        held = [(bits, tile) for (bits,), tile in zip(along_col, col_tiles)]
        for bits, tile in held:
            along_col.append((bits ^ (1 << power),))
            sent = saved_panels if tile is None else tile[0]
            if power == 0 and tile is None and len(held) > 1:
                sent = after(sent, held[-1][1])
            col_tiles.append(swap(sent, ("col",), sizes, {"col": 1 << power})[None])
    for bits in near:
        along_row.append((bits,))
        row_tiles.append(nearby[bits][None])
    if far:
        sent = jnp.stack(crossed)
        along_row.append(tuple(far))
        row_tiles.append(sent)
        for bits in near:
            along_row.append(tuple(other ^ bits for other in far))
            row_tiles.append(swap(sent, ("row",), sizes, {"row": bits}))

    arguments = (inverse_diag, cotangent, saved_panels, upstream, panel_tops)
    cot, saved, upstream_here, tops, solver = pl.pallas_call(
        prepare_kernel,
        out_shape=[jax.ShapeDtypeStruct(value.shape, BF16) for value in arguments[1:] + arguments[:1]],
        in_specs=[pl.BlockSpec(memory_space=pl.ANY)] * 5,
        out_specs=[VMEM] * 5,
        scratch_shapes=[pltpu.VMEM(inverse_diag.shape, F32), pltpu.SemaphoreType.DMA((5,))],
        compiler_params=limit,
    )(*[pltpu.with_memory_space_constraint(value, pltpu.HBM) for value in arguments])
    row_tiles[0] = saved[None]
    col_tiles[0] = saved[None]

    piece = panels * width // 8
    columns_keep, columns_send, keep, send = pl.pallas_call(
        functools.partial(main_kernel, along_row, along_col),
        out_shape=[
            jax.ShapeDtypeStruct((cols // 2, panels, height, width), F32),
            jax.ShapeDtypeStruct((cols // 2, panels, height, width), F32),
            jax.ShapeDtypeStruct((4, piece, width), F32),
            jax.ShapeDtypeStruct((4, piece, width), BF16),
        ],
        in_specs=[VMEM] * (len(row_tiles) + len(col_tiles) + 4),
        out_specs=[VMEM] * 4,
        scratch_shapes=[
            pltpu.VMEM((rows * height, panels * width), BF16),
            pltpu.VMEM((cols * height, panels * width), BF16),
            pltpu.VMEM((cols * height, panels * width), F32),
            pltpu.VMEM((panels * width, width), F32),
        ],
        compiler_params=limit,
    )(*row_tiles, *col_tiles, cot, upstream_here, solver, tops)

    both = ("row", "col")
    half = keep + swap(send, ("col",), sizes, {"col": 1}).astype(F32)
    spots = [{"col": (bits >> 1) * 2, "row": bits & 1} for bits in range(4)]
    total = half[0]
    for bits in (3, 1, 2):
        total = total + swap(half[bits].astype(BF16), both, sizes, spots[bits]).astype(F32)
    arrived = swap(columns_send, ("col",), sizes, {"col": 1})
    columns = columns_keep + arrived.astype(F32)
    for power in range(1, cols.bit_length() - 1):
        halves = columns.reshape(-1, 2, panels, height, width)
        arrived = swap(after(halves[:, 1].astype(BF16), half), ("col",), sizes, {"col": 1 << power})
        columns = halves[:, 0] + arrived.astype(F32)
    mine = total.astype(BF16)
    columns = columns[0].astype(BF16)

    others = [{"row": 1 << power} for power in range(1, rows.bit_length() - 1)]
    others += [{"col": 1 << power} for power in range(2, cols.bit_length() - 1)]
    if len(others) == 2 and "col" not in others[1]:
        first, second = others[0]["row"], others[1]["row"]
        from_first, from_second, from_both = [
            swap(mine, ("row",), sizes, {"row": bits}) for bits in (first, second, first ^ second)
        ]
        from_second, from_first, from_both, arrived = lax.optimization_barrier(
            (from_second, from_first, from_both, arrived)
        )
        total = (mine.astype(F32) + from_first.astype(F32)) + (
            from_second.astype(F32) + from_both.astype(F32)
        )
    else:
        for bits in others:
            total = mine.astype(F32) + swap(mine, tuple(bits), sizes, bits).astype(F32)
            mine = total.astype(BF16)
    mine = total.astype(BF16)
    here = jnp.stack([mine] + [swap(mine, both, sizes, spots[bits]) for bits in range(1, 4)])
    there = swap(here, ("col",), sizes, {"col": 1})
    diag_cot = pl.pallas_call(
        finish_kernel,
        out_shape=jax.ShapeDtypeStruct((panels * width, width), F32),
        in_specs=[VMEM] * 2,
        out_specs=VMEM,
        compiler_params=limit,
    )(here, there)
    return columns, diag_cot.reshape(panels, width, width)


def solution(mesh):
    in_specs = (
        P("row", "col"),
        P(None, ("row", "col"), None),
        P(None, ("row", "col"), None),
        P(),
        P(),
    )
    out_specs = (P(None, ("row", "col"), None), P())
    return jax.shard_map(
        functools.partial(body, dict(mesh.shape)),
        mesh=mesh,
        in_specs=in_specs,
        out_specs=out_specs,
        check_vma=False,
    )
```

```python
import functools

import jax
import jax.numpy as jnp
from jax import lax
from jax.experimental import pallas as pl
from jax.experimental.pallas import tpu as pltpu
from jax.sharding import PartitionSpec as P

F32 = jnp.float32
BF16 = jnp.bfloat16
VMEM = pl.BlockSpec(memory_space=pltpu.VMEM)


def swap(value, axes, sizes, bits):
    dims = [sizes[axis] for axis in axes]
    pairs = []
    count = 1
    for dim in dims:
        count *= dim
    for source in range(count):
        rest, coords = source, []
        for dim in reversed(dims):
            coords.append(rest % dim)
            rest //= dim
        coords = coords[::-1]
        target = 0
        for axis, dim, coord in zip(axes, dims, coords):
            target = target * dim + (coord ^ bits.get(axis, 0))
        pairs.append((source, target))
    return lax.ppermute(value, axes, pairs)


def dot(left, right):
    return jnp.dot(left, right, preferred_element_type=F32)


def dot_rows(left, right):
    return lax.dot_general(left, right, (((0,), (0,)), ((), ())), preferred_element_type=F32)


def prepare_kernel(*refs):
    sources, outs, (solver_out, solver, sems) = refs[:5], refs[5:9], refs[9:]
    copies = [
        pltpu.make_async_copy(source, target, sems.at[index])
        for index, (source, target) in enumerate(zip(sources, (solver, *outs)))
    ]
    for copy in copies:
        copy.start()
    copies[0].wait()
    solver_out[...] = solver[...].astype(BF16)
    for copy in copies[1:]:
        copy.wait()


def main_kernel(along_row, along_col, *refs):
    row_refs, refs = refs[: len(along_row)], refs[len(along_row) :]
    col_refs, refs = refs[: len(along_col)], refs[len(along_col) :]
    cot_ref, upstream_ref, solver_ref, tops_ref = refs[:4]
    columns_keep, columns_send, keep_ref, send_ref, joined, own, total, diag = refs[4:]
    row, col = lax.axis_index("row"), lax.axis_index("col")
    panels, height, width = upstream_ref.shape

    def place(target, index, tile):
        start = pl.multiple_of(index * height, height)
        for panel in range(panels):
            target[pl.ds(start, height), panel * width : (panel + 1) * width] = tile[panel]

    for bits_list, ref in zip(along_row, row_refs):
        for spot, bits in enumerate(bits_list):
            place(joined, row ^ bits, ref.at[spot])
    for bits_list, ref in zip(along_col, col_refs):
        for spot, bits in enumerate(bits_list):
            place(own, col ^ bits, ref.at[spot])
    total[...] = -2.0 * dot(cot_ref[...], joined[...])
    mine = pl.ds(pl.multiple_of(col * height, height), height)
    for index in range(panels):
        span = slice(index * width, (index + 1) * width)
        total[mine, span] += upstream_ref[index].astype(F32)

    columns = []
    tall = own.shape[0]
    for index in range(panels):
        span = slice(index * width, (index + 1) * width)
        panel = own[:, span]
        combined = total[:, span]
        appended = None
        for earlier in range(index):
            term = dot(columns[earlier], tops_ref[index * (index - 1) // 2 + earlier])
            appended = term if appended is None else appended + term
        if appended is not None:
            combined = combined - 2.0 * appended
        combined = combined.astype(BF16)
        if appended is None:
            now = dot(combined, solver_ref[index])
        else:
            solved = dot(jnp.concatenate([combined, panel]), solver_ref[index])
            now, solved = solved[:tall], 2.0 * solved[tall:]
        total[:, span] = now
        now = now.astype(BF16)
        columns.append(now)
        if appended is None:
            result = dot_rows(panel, -now)
        else:
            result = dot_rows(
                jnp.concatenate([panel, appended.astype(BF16)]),
                jnp.concatenate([-now, solved.astype(BF16)]),
            )
        diag[span, :] = result

    piece = keep_ref.shape[1]
    core, spot = place_of()
    for bits in range(4):
        here = pl.multiple_of((core * 4 + (spot ^ bits)) * piece, piece)
        there = pl.multiple_of(((1 - core) * 4 + (spot ^ bits)) * piece, piece)
        keep_ref[bits] = diag[pl.ds(here, piece), :]
        send_ref[bits] = diag[pl.ds(there, piece), :].astype(BF16)
    for pair in range(columns_keep.shape[0]):
        for bits, ref in ((2 * pair, columns_keep), (2 * pair + 1, columns_send)):
            tile = pl.ds(pl.multiple_of((col ^ bits) * height, height), height)
            for index in range(panels):
                ref[pair, index] = total[tile, index * width : (index + 1) * width].astype(ref.dtype)


def place_of():
    row, col = lax.axis_index("row"), lax.axis_index("col")
    return col & 1, ((col >> 1) & 1) * 2 + (row & 1)


def finish_kernel(here_ref, there_ref, out_ref):
    core, spot = place_of()
    piece = here_ref.shape[1]
    for bits in range(4):
        here = pl.multiple_of((core * 4 + (spot ^ bits)) * piece, piece)
        there = pl.multiple_of(((1 - core) * 4 + (spot ^ bits)) * piece, piece)
        out_ref[pl.ds(here, piece), :] = here_ref[bits].astype(F32)
        out_ref[pl.ds(there, piece), :] = there_ref[bits].astype(F32)


def after(value, *others):
    return lax.optimization_barrier((value, *others))[0]


def body(sizes, cotangent, saved_panels, upstream, inverse_diag, panel_tops):
    rows, cols = sizes["row"], sizes["col"]
    panels, height, width = saved_panels.shape
    limit = pltpu.CompilerParams(vmem_limit_bytes=32 * 1024 * 1024)
    tile_shape = jax.ShapeDtypeStruct(saved_panels.shape, BF16)

    near = [bits for bits in (2, 3, 1) if bits < rows]
    along_row, row_tiles = [(0,)], [None]
    far = [bits for bits in range(4, rows, 4)]
    crossed = [swap(saved_panels, ("row",), sizes, {"row": bits}) for bits in far]
    nearby = {bits: swap(saved_panels, ("row",), sizes, {"row": bits}) for bits in near}
    along_col = [(0,)]
    col_tiles = [None]
    for power in list(range(1, cols.bit_length() - 1)) + [0]:
        held = [(bits, tile) for (bits,), tile in zip(along_col, col_tiles)]
        for bits, tile in held:
            along_col.append((bits ^ (1 << power),))
            sent = saved_panels if tile is None else tile[0]
            if power == 0 and tile is None and len(held) > 1:
                sent = after(sent, held[-1][1])
            col_tiles.append(swap(sent, ("col",), sizes, {"col": 1 << power})[None])
    for bits in near:
        along_row.append((bits,))
        row_tiles.append(nearby[bits][None])
    if far:
        sent = jnp.stack(crossed)
        along_row.append(tuple(far))
        row_tiles.append(sent)
        for bits in near:
            along_row.append(tuple(other ^ bits for other in far))
            row_tiles.append(swap(sent, ("row",), sizes, {"row": bits}))

    arguments = (inverse_diag, cotangent, saved_panels, upstream, panel_tops)
    cot, saved, upstream_here, tops, solver = pl.pallas_call(
        prepare_kernel,
        out_shape=[jax.ShapeDtypeStruct(value.shape, BF16) for value in arguments[1:] + arguments[:1]],
        in_specs=[pl.BlockSpec(memory_space=pl.ANY)] * 5,
        out_specs=[VMEM] * 5,
        scratch_shapes=[pltpu.VMEM(inverse_diag.shape, F32), pltpu.SemaphoreType.DMA((5,))],
        compiler_params=limit,
    )(*[pltpu.with_memory_space_constraint(value, pltpu.HBM) for value in arguments])
    row_tiles[0] = saved[None]
    col_tiles[0] = saved[None]

    piece = panels * width // 8
    columns_keep, columns_send, keep, send = pl.pallas_call(
        functools.partial(main_kernel, along_row, along_col),
        out_shape=[
            jax.ShapeDtypeStruct((cols // 2, panels, height, width), F32),
            jax.ShapeDtypeStruct((cols // 2, panels, height, width), F32),
            jax.ShapeDtypeStruct((4, piece, width), F32),
            jax.ShapeDtypeStruct((4, piece, width), BF16),
        ],
        in_specs=[VMEM] * (len(row_tiles) + len(col_tiles) + 4),
        out_specs=[VMEM] * 4,
        scratch_shapes=[
            pltpu.VMEM((rows * height, panels * width), BF16),
            pltpu.VMEM((cols * height, panels * width), BF16),
            pltpu.VMEM((cols * height, panels * width), F32),
            pltpu.VMEM((panels * width, width), F32),
        ],
        compiler_params=limit,
    )(*row_tiles, *col_tiles, cot, upstream_here, solver, tops)

    both = ("row", "col")
    half = keep + swap(send, ("col",), sizes, {"col": 1}).astype(F32)
    spots = [{"col": (bits >> 1) * 2, "row": bits & 1} for bits in range(4)]
    total = half[0]
    for bits in (3, 1, 2):
        total = total + swap(half[bits].astype(BF16), both, sizes, spots[bits]).astype(F32)
    arrived = swap(columns_send, ("col",), sizes, {"col": 1})
    columns = columns_keep + arrived.astype(F32)
    for power in range(1, cols.bit_length() - 1):
        halves = columns.reshape(-1, 2, panels, height, width)
        arrived = swap(after(halves[:, 1].astype(BF16), half), ("col",), sizes, {"col": 1 << power})
        columns = halves[:, 0] + arrived.astype(F32)
    mine = total.astype(BF16)
    columns = columns[0].astype(BF16)

    others = [{"row": 1 << power} for power in range(1, rows.bit_length() - 1)]
    others += [{"col": 1 << power} for power in range(2, cols.bit_length() - 1)]
    if len(others) == 2 and "col" not in others[1]:
        first, second = others[0]["row"], others[1]["row"]
        from_first, from_second, from_both = [
            swap(mine, ("row",), sizes, {"row": bits}) for bits in (first, second, first ^ second)
        ]
        from_second, from_first, from_both, arrived = lax.optimization_barrier(
            (from_second, from_first, from_both, arrived)
        )
        total = (mine.astype(F32) + from_first.astype(F32)) + (
            from_second.astype(F32) + from_both.astype(F32)
        )
    else:
        for bits in others:
            total = mine.astype(F32) + swap(mine, tuple(bits), sizes, bits).astype(F32)
            mine = total.astype(BF16)
    mine = total.astype(BF16)
    here = jnp.stack([mine] + [swap(mine, both, sizes, spots[bits]) for bits in range(1, 4)])
    there = swap(here, ("col",), sizes, {"col": 1})
    diag_cot = pl.pallas_call(
        finish_kernel,
        out_shape=jax.ShapeDtypeStruct((panels * width, width), F32),
        in_specs=[VMEM] * 2,
        out_specs=VMEM,
        compiler_params=limit,
    )(here, there)
    return columns, diag_cot.reshape(panels, width, width)


def solution(mesh):
    in_specs = (
        P("row", "col"),
        P(None, ("row", "col"), None),
        P(None, ("row", "col"), None),
        P(),
        P(),
    )
    out_specs = (P(None, ("row", "col"), None), P())
    return jax.shard_map(
        functools.partial(body, dict(mesh.shape)),
        mesh=mesh,
        in_specs=in_specs,
        out_specs=out_specs,
        check_vma=False,
    )
```

```python
import functools

import jax
import jax.numpy as jnp
from jax import lax
from jax.experimental import pallas as pl
from jax.experimental.pallas import tpu as pltpu
from jax.sharding import PartitionSpec as P

F32 = jnp.float32
BF16 = jnp.bfloat16
VMEM = pl.BlockSpec(memory_space=pltpu.VMEM)


def swap(value, axes, sizes, bits):
    dims = [sizes[axis] for axis in axes]
    pairs = []
    count = 1
    for dim in dims:
        count *= dim
    for source in range(count):
        rest, coords = source, []
        for dim in reversed(dims):
            coords.append(rest % dim)
            rest //= dim
        coords = coords[::-1]
        target = 0
        for axis, dim, coord in zip(axes, dims, coords):
            target = target * dim + (coord ^ bits.get(axis, 0))
        pairs.append((source, target))
    return lax.ppermute(value, axes, pairs)


def dot(left, right):
    return jnp.dot(left, right, preferred_element_type=F32)


def dot_rows(left, right):
    return lax.dot_general(left, right, (((0,), (0,)), ((), ())), preferred_element_type=F32)


def prepare_kernel(*refs):
    sources, outs, (solver_out, solver, sems) = refs[:5], refs[5:9], refs[9:]
    copies = [
        pltpu.make_async_copy(source, target, sems.at[index])
        for index, (source, target) in enumerate(zip(sources, (solver, *outs)))
    ]
    for copy in copies:
        copy.start()
    copies[0].wait()
    solver_out[...] = solver[...].astype(BF16)
    for copy in copies[1:]:
        copy.wait()


def partner(row):
    return row ^ (1 + 2 * (row & 1))


def main_kernel(along_row, shared, along_col, *refs):
    shared_refs, refs = refs[: len(shared)], refs[len(shared) :]
    row_refs, refs = refs[: len(along_row)], refs[len(along_row) :]
    col_refs, refs = refs[: len(along_col)], refs[len(along_col) :]
    cot_ref, upstream_ref, solver_ref, tops_ref = refs[:4]
    columns_keep, columns_send, keep_ref, send_ref = refs[4:8]
    guests = [bits for bits_list in shared for bits in bits_list]
    back_refs, (joined, own, total, across, diag) = refs[8 : 8 + len(guests)], refs[8 + len(guests) :]
    row, col = lax.axis_index("row"), lax.axis_index("col")
    panels, height, width = upstream_ref.shape

    def place(target, index, tile):
        start = pl.multiple_of(index * height, height)
        for panel in range(panels):
            target[pl.ds(start, height), panel * width : (panel + 1) * width] = tile[panel]

    for bits_list, ref in zip(along_row, row_refs):
        for spot, bits in enumerate(bits_list):
            place(joined, row ^ bits, ref.at[spot])
    def tile_rows(index):
        return pl.ds(pl.multiple_of(index * height, height), height)

    base = len(along_col)
    tall = base * height
    for bits_list, ref in zip(along_col, col_refs):
        for spot, bits in enumerate(bits_list):
            place(own, col ^ bits, ref.at[spot])
    for bits_list, ref in zip(shared, shared_refs):
        for spot, bits in enumerate(bits_list):
            place(joined, partner(row) ^ bits, ref.at[spot])
            place(own, base + guests.index(bits), ref.at[spot])
            joined[tile_rows(partner(row) ^ bits ^ 2), :] = jnp.zeros((height, joined.shape[1]), BF16)
    total[:tall, :] = -2.0 * dot(cot_ref[...], joined[...])
    across[...] = -2.0 * dot_rows(cot_ref[...], own[:tall, :])
    for spot, bits in enumerate(guests):
        total[tall + spot * height : tall + (spot + 1) * height, :] = across[tile_rows(partner(row) ^ bits), :]
    mine = tile_rows(col)
    for index in range(panels):
        span = slice(index * width, (index + 1) * width)
        total[mine, span] += upstream_ref[index].astype(F32)

    columns = []
    tall = own.shape[0]
    for index in range(panels):
        span = slice(index * width, (index + 1) * width)
        panel = own[:, span]
        combined = total[:, span]
        appended = None
        for earlier in range(index):
            term = dot(columns[earlier], tops_ref[index * (index - 1) // 2 + earlier])
            appended = term if appended is None else appended + term
        if appended is not None:
            combined = combined - 2.0 * appended
        combined = combined.astype(BF16)
        if appended is None:
            now = dot(combined, solver_ref[index])
        else:
            solved = dot(jnp.concatenate([combined, panel]), solver_ref[index])
            now, solved = solved[:tall], 2.0 * solved[tall:]
        total[:, span] = now
        now = now.astype(BF16)
        columns.append(now)
        if appended is None:
            result = dot_rows(panel, -now)
        else:
            result = dot_rows(
                jnp.concatenate([panel, appended.astype(BF16)]),
                jnp.concatenate([-now, solved.astype(BF16)]),
            )
        diag[span, :] = result

    piece = keep_ref.shape[1]
    core, spot = place_of()
    for bits in range(4):
        here = pl.multiple_of((core * 4 + (spot ^ bits)) * piece, piece)
        there = pl.multiple_of(((1 - core) * 4 + (spot ^ bits)) * piece, piece)
        keep_ref[bits] = diag[pl.ds(here, piece), :]
        send_ref[bits] = diag[pl.ds(there, piece), :].astype(BF16)
    for pair in range(columns_keep.shape[0]):
        for bits, ref in ((2 * pair, columns_keep), (2 * pair + 1, columns_send)):
            tile = pl.ds(pl.multiple_of((col ^ bits) * height, height), height)
            for index in range(panels):
                ref[pair, index] = total[tile, index * width : (index + 1) * width].astype(ref.dtype)
    for spot, ref in enumerate(back_refs):
        start = (base + spot) * height
        for index in range(panels):
            tile = total[start : start + height, index * width : (index + 1) * width]
            ref[index] = tile.astype(BF16)


def place_of():
    row, col = lax.axis_index("row"), lax.axis_index("col")
    return col & 1, ((col >> 1) & 1) * 2 + (row & 1)


def finish_kernel(here_ref, there_ref, out_ref):
    core, spot = place_of()
    piece = here_ref.shape[1]
    for bits in range(4):
        here = pl.multiple_of((core * 4 + (spot ^ bits)) * piece, piece)
        there = pl.multiple_of(((1 - core) * 4 + (spot ^ bits)) * piece, piece)
        out_ref[pl.ds(here, piece), :] = here_ref[bits].astype(F32)
        out_ref[pl.ds(there, piece), :] = there_ref[bits].astype(F32)


def after(value, *others):
    return lax.optimization_barrier((value, *others))[0]


def body(sizes, cotangent, saved_panels, upstream, inverse_diag, panel_tops):
    rows, cols = sizes["row"], sizes["col"]
    panels, height, width = saved_panels.shape
    limit = pltpu.CompilerParams(vmem_limit_bytes=32 * 1024 * 1024)
    tile_shape = jax.ShapeDtypeStruct(saved_panels.shape, BF16)

    far = [bits for bits in range(4, rows, 4)]

    def guest(value, bits=0, back=False):
        pairs = [(partner(row) ^ bits, row) for row in range(rows)]
        return lax.ppermute(value, "row", [pair[::-1] for pair in pairs] if back else pairs)

    crossed = [swap(saved_panels, ("row",), sizes, {"row": bits}) for bits in far]
    along_row, row_tiles = [(0,), (2,)], [None, swap(saved_panels, ("row",), sizes, {"row": 2})[None]]
    shared, shared_tiles = [(0,)], [guest(saved_panels)[None]]
    along_col = [(0,)]
    col_tiles = [None]
    for power in list(range(1, cols.bit_length() - 1)) + [0]:
        held = [(bits, tile) for (bits,), tile in zip(along_col, col_tiles)]
        for bits, tile in held:
            along_col.append((bits ^ (1 << power),))
            sent = saved_panels if tile is None else tile[0]
            if power == 0 and tile is None and len(held) > 1:
                sent = after(sent, held[-1][1])
            col_tiles.append(swap(sent, ("col",), sizes, {"col": 1 << power})[None])
    if far:
        sent = jnp.stack(crossed)
        along_row.append(tuple(far))
        row_tiles.append(sent)
        for bits in (1, 2, 3):
            along_row.append(tuple(other ^ bits for other in far))
            row_tiles.append(swap(sent, ("row",), sizes, {"row": bits}))

    arguments = (inverse_diag, cotangent, saved_panels, upstream, panel_tops)
    cot, saved, upstream_here, tops, solver = pl.pallas_call(
        prepare_kernel,
        out_shape=[jax.ShapeDtypeStruct(value.shape, BF16) for value in arguments[1:] + arguments[:1]],
        in_specs=[pl.BlockSpec(memory_space=pl.ANY)] * 5,
        out_specs=[VMEM] * 5,
        scratch_shapes=[pltpu.VMEM(inverse_diag.shape, F32), pltpu.SemaphoreType.DMA((5,))],
        compiler_params=limit,
    )(*[pltpu.with_memory_space_constraint(value, pltpu.HBM) for value in arguments])
    row_tiles[0] = saved[None]
    col_tiles[0] = saved[None]

    piece = panels * width // 8
    tall = (cols + 1) * height
    columns_keep, columns_send, keep, send, *backs = pl.pallas_call(
        functools.partial(main_kernel, along_row, shared, along_col),
        out_shape=[
            jax.ShapeDtypeStruct((cols // 2, panels, height, width), F32),
            jax.ShapeDtypeStruct((cols // 2, panels, height, width), F32),
            jax.ShapeDtypeStruct((4, piece, width), F32),
            jax.ShapeDtypeStruct((4, piece, width), BF16),
        ]
        + [tile_shape],
        in_specs=[VMEM] * (len(row_tiles) + len(shared_tiles) + len(col_tiles) + 4),
        out_specs=[VMEM] * 5,
        scratch_shapes=[
            pltpu.VMEM((rows * height, panels * width), BF16),
            pltpu.VMEM((tall, panels * width), BF16),
            pltpu.VMEM((tall, panels * width), F32),
            pltpu.VMEM((rows * height, panels * width), F32),
            pltpu.VMEM((panels * width, width), F32),
        ],
        compiler_params=limit,
    )(*shared_tiles, *row_tiles, *col_tiles, cot, upstream_here, solver, tops)

    both = ("row", "col")
    half = keep + swap(send, ("col",), sizes, {"col": 1}).astype(F32)
    spots = [{"col": (bits >> 1) * 2, "row": bits & 1} for bits in range(4)]
    total = half[0]
    for bits in (3, 1, 2):
        total = total + swap(half[bits].astype(BF16), both, sizes, spots[bits]).astype(F32)
    returned = guest(after(backs[0], half), back=True)
    arrived = swap(columns_send, ("col",), sizes, {"col": 1})
    columns = columns_keep + arrived.astype(F32)
    for power in range(1, cols.bit_length() - 1):
        halves = columns.reshape(-1, 2, panels, height, width)
        arrived = swap(after(halves[:, 1].astype(BF16), half), ("col",), sizes, {"col": 1 << power})
        columns = halves[:, 0] + arrived.astype(F32)
    mine = total.astype(BF16)
    columns = columns[0]
    columns = (columns + returned.astype(F32)).astype(BF16)

    others = [{"row": 1 << power} for power in range(1, rows.bit_length() - 1)]
    others += [{"col": 1 << power} for power in range(2, cols.bit_length() - 1)]
    if len(others) == 2 and "col" not in others[1]:
        first, second = others[0]["row"], others[1]["row"]
        from_first, from_second, from_both = [
            swap(mine, ("row",), sizes, {"row": bits}) for bits in (first, second, first ^ second)
        ]
        from_second, from_first, from_both, arrived, returned = lax.optimization_barrier(
            (from_second, from_first, from_both, arrived, returned)
        )
        total = (mine.astype(F32) + from_first.astype(F32)) + (
            from_second.astype(F32) + from_both.astype(F32)
        )
    else:
        for bits in others:
            total = mine.astype(F32) + swap(mine, tuple(bits), sizes, bits).astype(F32)
            mine = total.astype(BF16)
    mine = total.astype(BF16)
    here = jnp.stack([mine] + [swap(mine, both, sizes, spots[bits]) for bits in range(1, 4)])
    there = swap(here, ("col",), sizes, {"col": 1})
    diag_cot = pl.pallas_call(
        finish_kernel,
        out_shape=jax.ShapeDtypeStruct((panels * width, width), F32),
        in_specs=[VMEM] * 2,
        out_specs=VMEM,
        compiler_params=limit,
    )(here, there)
    return columns, diag_cot.reshape(panels, width, width)


def solution(mesh):
    in_specs = (
        P("row", "col"),
        P(None, ("row", "col"), None),
        P(None, ("row", "col"), None),
        P(),
        P(),
    )
    out_specs = (P(None, ("row", "col"), None), P())
    return jax.shard_map(
        functools.partial(body, dict(mesh.shape)),
        mesh=mesh,
        in_specs=in_specs,
        out_specs=out_specs,
        check_vma=False,
    )
```

```python
import functools

import jax
import jax.numpy as jnp
from jax import lax
from jax.experimental import pallas as pl
from jax.experimental.pallas import tpu as pltpu
from jax.sharding import PartitionSpec as P

F32 = jnp.float32
BF16 = jnp.bfloat16
VMEM = pl.BlockSpec(memory_space=pltpu.VMEM)


def swap(value, axes, sizes, bits):
    dims = [sizes[axis] for axis in axes]
    pairs = []
    count = 1
    for dim in dims:
        count *= dim
    for source in range(count):
        rest, coords = source, []
        for dim in reversed(dims):
            coords.append(rest % dim)
            rest //= dim
        coords = coords[::-1]
        target = 0
        for axis, dim, coord in zip(axes, dims, coords):
            target = target * dim + (coord ^ bits.get(axis, 0))
        pairs.append((source, target))
    return lax.ppermute(value, axes, pairs)


def dot(left, right):
    return jnp.dot(left, right, preferred_element_type=F32)


def dot_rows(left, right):
    return lax.dot_general(left, right, (((0,), (0,)), ((), ())), preferred_element_type=F32)


def prepare_kernel(*refs):
    sources, outs, (solver_out, solver, sems) = refs[:5], refs[5:9], refs[9:]
    copies = [
        pltpu.make_async_copy(source, target, sems.at[index])
        for index, (source, target) in enumerate(zip(sources, (solver, *outs)))
    ]
    for copy in copies:
        copy.start()
    copies[0].wait()
    solver_out[...] = solver[...].astype(BF16)
    for copy in copies[1:]:
        copy.wait()


def main_kernel(along_row, along_col, *refs):
    row_refs, refs = refs[: len(along_row)], refs[len(along_row) :]
    col_refs, refs = refs[: len(along_col)], refs[len(along_col) :]
    cot_ref, upstream_ref, solver_ref, tops_ref = refs[:4]
    columns_keep, columns_send, keep_ref, send_ref, joined, own, total, diag = refs[4:]
    row, col = lax.axis_index("row"), lax.axis_index("col")
    panels, height, width = upstream_ref.shape

    def place(target, index, tile):
        start = pl.multiple_of(index * height, height)
        for panel in range(panels):
            target[pl.ds(start, height), panel * width : (panel + 1) * width] = tile[panel]

    for bits_list, ref in zip(along_row, row_refs):
        for spot, bits in enumerate(bits_list):
            place(joined, row ^ bits, ref.at[spot])
    for bits_list, ref in zip(along_col, col_refs):
        for spot, bits in enumerate(bits_list):
            place(own, col ^ bits, ref.at[spot])
    total[...] = -2.0 * dot(cot_ref[...], joined[...])
    mine = pl.ds(pl.multiple_of(col * height, height), height)
    for index in range(panels):
        span = slice(index * width, (index + 1) * width)
        total[mine, span] += upstream_ref[index].astype(F32)

    columns = []
    tall = own.shape[0]
    for index in range(panels):
        span = slice(index * width, (index + 1) * width)
        panel = own[:, span]
        combined = total[:, span]
        appended = None
        for earlier in range(index):
            term = dot(columns[earlier], tops_ref[index * (index - 1) // 2 + earlier])
            appended = term if appended is None else appended + term
        if appended is not None:
            combined = combined - 2.0 * appended
        combined = combined.astype(BF16)
        if appended is None:
            now = dot(combined, solver_ref[index])
        else:
            solved = dot(jnp.concatenate([combined, panel]), solver_ref[index])
            now, solved = solved[:tall], 2.0 * solved[tall:]
        total[:, span] = now
        now = now.astype(BF16)
        columns.append(now)
        if appended is None:
            result = dot_rows(panel, -now)
        else:
            result = dot_rows(
                jnp.concatenate([panel, appended.astype(BF16)]),
                jnp.concatenate([-now, solved.astype(BF16)]),
            )
        diag[span, :] = result

    piece = keep_ref.shape[1]
    core, spot = place_of()
    for bits in range(4):
        here = pl.multiple_of((core * 4 + (spot ^ bits)) * piece, piece)
        there = pl.multiple_of(((1 - core) * 4 + (spot ^ bits)) * piece, piece)
        keep_ref[bits] = diag[pl.ds(here, piece), :]
        send_ref[bits] = diag[pl.ds(there, piece), :].astype(BF16)
    for pair in range(columns_keep.shape[0]):
        for bits, ref in ((2 * pair, columns_keep), (2 * pair + 1, columns_send)):
            tile = pl.ds(pl.multiple_of((col ^ bits) * height, height), height)
            for index in range(panels):
                ref[pair, index] = total[tile, index * width : (index + 1) * width].astype(ref.dtype)


def place_of():
    row, col = lax.axis_index("row"), lax.axis_index("col")
    return col & 1, ((col >> 1) & 1) * 2 + (row & 1)


def finish_kernel(here_ref, there_ref, out_ref):
    core, spot = place_of()
    piece = here_ref.shape[1]
    for bits in range(4):
        here = pl.multiple_of((core * 4 + (spot ^ bits)) * piece, piece)
        there = pl.multiple_of(((1 - core) * 4 + (spot ^ bits)) * piece, piece)
        out_ref[pl.ds(here, piece), :] = here_ref[bits].astype(F32)
        out_ref[pl.ds(there, piece), :] = there_ref[bits].astype(F32)


def after(value, *others):
    return lax.optimization_barrier((value, *others))[0]


def body(sizes, cotangent, saved_panels, upstream, inverse_diag, panel_tops):
    rows, cols = sizes["row"], sizes["col"]
    panels, height, width = saved_panels.shape
    limit = pltpu.CompilerParams(vmem_limit_bytes=32 * 1024 * 1024)
    tile_shape = jax.ShapeDtypeStruct(saved_panels.shape, BF16)

    near = [bits for bits in (2, 1, 3) if bits < rows]
    along_row, row_tiles = [(0,)], [None]
    far = [bits for bits in range(4, rows, 4)]
    crossed = [swap(saved_panels, ("row",), sizes, {"row": bits}) for bits in far]
    nearby = {bits: swap(saved_panels, ("row",), sizes, {"row": bits}) for bits in near}
    along_col = [(0,)]
    col_tiles = [None]
    for power in list(range(1, cols.bit_length() - 1)) + [0]:
        held = [(bits, tile) for (bits,), tile in zip(along_col, col_tiles)]
        for bits, tile in held:
            along_col.append((bits ^ (1 << power),))
            sent = saved_panels if tile is None else tile[0]
            if power == 0 and tile is None and len(held) > 1:
                sent = after(sent, held[-1][1])
            col_tiles.append(swap(sent, ("col",), sizes, {"col": 1 << power})[None])
    for bits in near:
        along_row.append((bits,))
        row_tiles.append(nearby[bits][None])
    if far:
        sent = jnp.stack(crossed)
        along_row.append(tuple(far))
        row_tiles.append(sent)
        for bits in near:
            along_row.append(tuple(other ^ bits for other in far))
            row_tiles.append(swap(sent, ("row",), sizes, {"row": bits}))

    arguments = (inverse_diag, cotangent, saved_panels, upstream, panel_tops)
    cot, saved, upstream_here, tops, solver = pl.pallas_call(
        prepare_kernel,
        out_shape=[jax.ShapeDtypeStruct(value.shape, BF16) for value in arguments[1:] + arguments[:1]],
        in_specs=[pl.BlockSpec(memory_space=pl.ANY)] * 5,
        out_specs=[VMEM] * 5,
        scratch_shapes=[pltpu.VMEM(inverse_diag.shape, F32), pltpu.SemaphoreType.DMA((5,))],
        compiler_params=limit,
    )(*[pltpu.with_memory_space_constraint(value, pltpu.HBM) for value in arguments])
    row_tiles[0] = saved[None]
    col_tiles[0] = saved[None]

    piece = panels * width // 8
    columns_keep, columns_send, keep, send = pl.pallas_call(
        functools.partial(main_kernel, along_row, along_col),
        out_shape=[
            jax.ShapeDtypeStruct((cols // 2, panels, height, width), F32),
            jax.ShapeDtypeStruct((cols // 2, panels, height, width), F32),
            jax.ShapeDtypeStruct((4, piece, width), F32),
            jax.ShapeDtypeStruct((4, piece, width), BF16),
        ],
        in_specs=[VMEM] * (len(row_tiles) + len(col_tiles) + 4),
        out_specs=[VMEM] * 4,
        scratch_shapes=[
            pltpu.VMEM((rows * height, panels * width), BF16),
            pltpu.VMEM((cols * height, panels * width), BF16),
            pltpu.VMEM((cols * height, panels * width), F32),
            pltpu.VMEM((panels * width, width), F32),
        ],
        compiler_params=limit,
    )(*row_tiles, *col_tiles, cot, upstream_here, solver, tops)

    both = ("row", "col")
    half = keep + swap(send, ("col",), sizes, {"col": 1}).astype(F32)
    spots = [{"col": (bits >> 1) * 2, "row": bits & 1} for bits in range(4)]
    total = half[0]
    for bits in (3, 1, 2):
        total = total + swap(half[bits].astype(BF16), both, sizes, spots[bits]).astype(F32)
    arrived = swap(columns_send, ("col",), sizes, {"col": 1})
    columns = columns_keep + arrived.astype(F32)
    for power in range(1, cols.bit_length() - 1):
        halves = columns.reshape(-1, 2, panels, height, width)
        arrived = swap(after(halves[:, 1].astype(BF16), half), ("col",), sizes, {"col": 1 << power})
        columns = halves[:, 0] + arrived.astype(F32)
    mine = total.astype(BF16)
    columns = columns[0].astype(BF16)

    others = [{"row": 1 << power} for power in range(1, rows.bit_length() - 1)]
    others += [{"col": 1 << power} for power in range(2, cols.bit_length() - 1)]
    if len(others) == 2 and "col" not in others[1]:
        first, second = others[0]["row"], others[1]["row"]
        from_first, from_second, from_both = [
            swap(mine, ("row",), sizes, {"row": bits}) for bits in (first, second, first ^ second)
        ]
        from_second, from_first, from_both, arrived = lax.optimization_barrier(
            (from_second, from_first, from_both, arrived)
        )
        total = (mine.astype(F32) + from_first.astype(F32)) + (
            from_second.astype(F32) + from_both.astype(F32)
        )
    else:
        for bits in others:
            total = mine.astype(F32) + swap(mine, tuple(bits), sizes, bits).astype(F32)
            mine = total.astype(BF16)
    mine = total.astype(BF16)
    here = jnp.stack([mine] + [swap(mine, both, sizes, spots[bits]) for bits in range(1, 4)])
    there = swap(here, ("col",), sizes, {"col": 1})
    diag_cot = pl.pallas_call(
        finish_kernel,
        out_shape=jax.ShapeDtypeStruct((panels * width, width), F32),
        in_specs=[VMEM] * 2,
        out_specs=VMEM,
        compiler_params=limit,
    )(here, there)
    return columns, diag_cot.reshape(panels, width, width)


def solution(mesh):
    in_specs = (
        P("row", "col"),
        P(None, ("row", "col"), None),
        P(None, ("row", "col"), None),
        P(),
        P(),
    )
    out_specs = (P(None, ("row", "col"), None), P())
    return jax.shard_map(
        functools.partial(body, dict(mesh.shape)),
        mesh=mesh,
        in_specs=in_specs,
        out_specs=out_specs,
        check_vma=False,
    )
```

```python
import functools

import jax
import jax.numpy as jnp
from jax import lax
from jax.experimental import pallas as pl
from jax.experimental.pallas import tpu as pltpu
from jax.sharding import PartitionSpec as P

F32 = jnp.float32
BF16 = jnp.bfloat16
VMEM = pl.BlockSpec(memory_space=pltpu.VMEM)


def swap(value, axes, sizes, bits):
    dims = [sizes[axis] for axis in axes]
    pairs = []
    count = 1
    for dim in dims:
        count *= dim
    for source in range(count):
        rest, coords = source, []
        for dim in reversed(dims):
            coords.append(rest % dim)
            rest //= dim
        coords = coords[::-1]
        target = 0
        for axis, dim, coord in zip(axes, dims, coords):
            target = target * dim + (coord ^ bits.get(axis, 0))
        pairs.append((source, target))
    return lax.ppermute(value, axes, pairs)


def dot(left, right):
    return jnp.dot(left, right, preferred_element_type=F32)


def dot_rows(left, right):
    return lax.dot_general(left, right, (((0,), (0,)), ((), ())), preferred_element_type=F32)


def prepare_kernel(*refs):
    sources, outs, (solver_out, solver, sems) = refs[:5], refs[5:9], refs[9:]
    copies = [
        pltpu.make_async_copy(source, target, sems.at[index])
        for index, (source, target) in enumerate(zip(sources, (solver, *outs)))
    ]
    for copy in copies:
        copy.start()
    copies[0].wait()
    solver_out[...] = solver[...].astype(BF16)
    for copy in copies[1:]:
        copy.wait()


def main_kernel(along_row, along_col, *refs):
    row_refs, refs = refs[: len(along_row)], refs[len(along_row) :]
    col_refs, refs = refs[: len(along_col)], refs[len(along_col) :]
    cot_ref, upstream_ref, solver_ref, tops_ref = refs[:4]
    columns_keep, columns_send, keep_ref, send_ref, joined, own, total, diag = refs[4:]
    row, col = lax.axis_index("row"), lax.axis_index("col")
    panels, height, width = upstream_ref.shape

    def place(target, index, tile):
        start = pl.multiple_of(index * height, height)
        for panel in range(panels):
            target[pl.ds(start, height), panel * width : (panel + 1) * width] = tile[panel]

    for bits_list, ref in zip(along_row, row_refs):
        for spot, bits in enumerate(bits_list):
            place(joined, row ^ bits, ref.at[spot])
    for bits_list, ref in zip(along_col, col_refs):
        for spot, bits in enumerate(bits_list):
            place(own, col ^ bits, ref.at[spot])
    total[...] = -2.0 * dot(cot_ref[...], joined[...])
    mine = pl.ds(pl.multiple_of(col * height, height), height)
    for index in range(panels):
        span = slice(index * width, (index + 1) * width)
        total[mine, span] += upstream_ref[index].astype(F32)

    columns = []
    tall = own.shape[0]
    for index in range(panels):
        span = slice(index * width, (index + 1) * width)
        panel = own[:, span]
        combined = total[:, span]
        appended = None
        for earlier in range(index):
            term = dot(columns[earlier], tops_ref[index * (index - 1) // 2 + earlier])
            appended = term if appended is None else appended + term
        if appended is not None:
            combined = combined - 2.0 * appended
        combined = combined.astype(BF16)
        if appended is None:
            now = dot(combined, solver_ref[index])
        else:
            solved = dot(jnp.concatenate([combined, panel]), solver_ref[index])
            now, solved = solved[:tall], 2.0 * solved[tall:]
        total[:, span] = now
        now = now.astype(BF16)
        columns.append(now)
        if appended is None:
            result = dot_rows(panel, -now)
        else:
            result = dot_rows(
                jnp.concatenate([panel, appended.astype(BF16)]),
                jnp.concatenate([-now, solved.astype(BF16)]),
            )
        diag[span, :] = result

    piece = keep_ref.shape[1]
    core, spot = place_of()
    for bits in range(4):
        here = pl.multiple_of((core * 4 + (spot ^ bits)) * piece, piece)
        there = pl.multiple_of(((1 - core) * 4 + (spot ^ bits)) * piece, piece)
        keep_ref[bits] = diag[pl.ds(here, piece), :]
        send_ref[bits] = diag[pl.ds(there, piece), :].astype(BF16)
    for pair in range(columns_keep.shape[0]):
        for bits, ref in ((2 * pair, columns_keep), (2 * pair + 1, columns_send)):
            tile = pl.ds(pl.multiple_of((col ^ bits) * height, height), height)
            for index in range(panels):
                ref[pair, index] = total[tile, index * width : (index + 1) * width].astype(ref.dtype)


def place_of():
    row, col = lax.axis_index("row"), lax.axis_index("col")
    return col & 1, ((col >> 1) & 1) * 2 + (row & 1)


def finish_kernel(here_ref, there_ref, out_ref):
    core, spot = place_of()
    piece = here_ref.shape[1]
    for bits in range(4):
        here = pl.multiple_of((core * 4 + (spot ^ bits)) * piece, piece)
        there = pl.multiple_of(((1 - core) * 4 + (spot ^ bits)) * piece, piece)
        out_ref[pl.ds(here, piece), :] = here_ref[bits].astype(F32)
        out_ref[pl.ds(there, piece), :] = there_ref[bits].astype(F32)


def after(value, *others):
    return lax.optimization_barrier((value, *others))[0]


def body(sizes, cotangent, saved_panels, upstream, inverse_diag, panel_tops):
    rows, cols = sizes["row"], sizes["col"]
    panels, height, width = saved_panels.shape
    limit = pltpu.CompilerParams(vmem_limit_bytes=32 * 1024 * 1024)
    tile_shape = jax.ShapeDtypeStruct(saved_panels.shape, BF16)

    near = [bits for bits in (2, 3, 1) if bits < rows]
    along_row, row_tiles = [(0,)], [None]
    far = [bits for bits in range(4, rows, 4)]
    crossed = [swap(saved_panels, ("row",), sizes, {"row": bits}) for bits in far]
    nearby = {bits: swap(saved_panels, ("row",), sizes, {"row": bits}) for bits in near}
    along_col = [(0,)]
    col_tiles = [None]
    for power in list(range(1, cols.bit_length() - 1)) + [0]:
        held = [(bits, tile) for (bits,), tile in zip(along_col, col_tiles)]
        for bits, tile in held:
            along_col.append((bits ^ (1 << power),))
            sent = saved_panels if tile is None else tile[0]
            if power == 0 and tile is None and len(held) > 1:
                sent = after(sent, held[-1][1])
            col_tiles.append(swap(sent, ("col",), sizes, {"col": 1 << power})[None])
    for bits in near:
        along_row.append((bits,))
        row_tiles.append(nearby[bits][None])
    if far:
        sent = jnp.stack(crossed)
        along_row.append(tuple(far))
        row_tiles.append(sent)
        for bits in near:
            along_row.append(tuple(other ^ bits for other in far))
            row_tiles.append(swap(sent, ("row",), sizes, {"row": bits}))

    arguments = (inverse_diag, cotangent, saved_panels, upstream, panel_tops)
    cot, saved, upstream_here, tops, solver = pl.pallas_call(
        prepare_kernel,
        out_shape=[jax.ShapeDtypeStruct(value.shape, BF16) for value in arguments[1:] + arguments[:1]],
        in_specs=[pl.BlockSpec(memory_space=pl.ANY)] * 5,
        out_specs=[VMEM] * 5,
        scratch_shapes=[pltpu.VMEM(inverse_diag.shape, F32), pltpu.SemaphoreType.DMA((5,))],
        compiler_params=limit,
    )(*[pltpu.with_memory_space_constraint(value, pltpu.HBM) for value in arguments])
    row_tiles[0] = saved[None]
    col_tiles[0] = saved[None]

    piece = panels * width // 8
    columns_keep, columns_send, keep, send = pl.pallas_call(
        functools.partial(main_kernel, along_row, along_col),
        out_shape=[
            jax.ShapeDtypeStruct((cols // 2, panels, height, width), F32),
            jax.ShapeDtypeStruct((cols // 2, panels, height, width), F32),
            jax.ShapeDtypeStruct((4, piece, width), F32),
            jax.ShapeDtypeStruct((4, piece, width), BF16),
        ],
        in_specs=[VMEM] * (len(row_tiles) + len(col_tiles) + 4),
        out_specs=[VMEM] * 4,
        scratch_shapes=[
            pltpu.VMEM((rows * height, panels * width), BF16),
            pltpu.VMEM((cols * height, panels * width), BF16),
            pltpu.VMEM((cols * height, panels * width), F32),
            pltpu.VMEM((panels * width, width), F32),
        ],
        compiler_params=limit,
    )(*row_tiles, *col_tiles, cot, upstream_here, solver, tops)

    both = ("row", "col")
    half = keep + swap(send, ("col",), sizes, {"col": 1}).astype(F32)
    spots = [{"col": (bits >> 1) * 2, "row": bits & 1} for bits in range(4)]
    total = half[0]
    for bits in (3, 1, 2):
        total = total + swap(half[bits].astype(BF16), both, sizes, spots[bits]).astype(F32)
    arrived = swap(columns_send, ("col",), sizes, {"col": 1})
    columns = columns_keep + arrived.astype(F32)
    for power in range(1, cols.bit_length() - 1):
        halves = columns.reshape(-1, 2, panels, height, width)
        arrived = swap(after(halves[:, 1].astype(BF16), half), ("col",), sizes, {"col": 1 << power})
        columns = halves[:, 0] + arrived.astype(F32)
    mine = total.astype(BF16)
    columns = columns[0].astype(BF16)

    others = [{"row": 1 << power} for power in range(1, rows.bit_length() - 1)]
    others += [{"col": 1 << power} for power in range(2, cols.bit_length() - 1)]
    if len(others) == 2 and "col" not in others[1]:
        first, second = others[0]["row"], others[1]["row"]
        from_first, from_second, from_both = [
            swap(mine, ("row",), sizes, {"row": bits}) for bits in (first, second, first ^ second)
        ]
        arrived, from_first, from_second, from_both = lax.optimization_barrier(
            (arrived, from_first, from_second, from_both)
        )
        total = (mine.astype(F32) + from_first.astype(F32)) + (
            from_second.astype(F32) + from_both.astype(F32)
        )
    else:
        for bits in others:
            total = mine.astype(F32) + swap(mine, tuple(bits), sizes, bits).astype(F32)
            mine = total.astype(BF16)
    mine = total.astype(BF16)
    here = jnp.stack([mine] + [swap(mine, both, sizes, spots[bits]) for bits in range(1, 4)])
    there = swap(here, ("col",), sizes, {"col": 1})
    diag_cot = pl.pallas_call(
        finish_kernel,
        out_shape=jax.ShapeDtypeStruct((panels * width, width), F32),
        in_specs=[VMEM] * 2,
        out_specs=VMEM,
        compiler_params=limit,
    )(here, there)
    return columns, diag_cot.reshape(panels, width, width)


def solution(mesh):
    in_specs = (
        P("row", "col"),
        P(None, ("row", "col"), None),
        P(None, ("row", "col"), None),
        P(),
        P(),
    )
    out_specs = (P(None, ("row", "col"), None), P())
    return jax.shard_map(
        functools.partial(body, dict(mesh.shape)),
        mesh=mesh,
        in_specs=in_specs,
        out_specs=out_specs,
        check_vma=False,
    )
```
